512 devices in a mesh: dom: 128 (over z, y, core), sub: 4 (over x).
Axes of the slice: x: 4, y: 8, z: 8, core: 2. Of those that a mesh axis runs over, the one named last changes fastest.
Arguments:
- rhs: float32 [64, 8, 65536], P(None, None, ('dom', 'sub')), may hold values from -6 to 6
- guess: float32 [64, 8, 65536], P(None, None, ('dom', 'sub')), may hold values from -4 to 4
- diag_blocks: bfloat16 [2, 64, 64], replicated
- face_blocks: bfloat16 [6, 2, 64, 64], replicated, may hold values from -0.3125 to 0.3125
- smoother: bfloat16 [2, 64, 64], replicated
- coarse_inverse: bfloat16 [64, 64], replicated
- elem_type: int32 [65536], P(('dom', 'sub')), may hold values from 0 to 1
- face_type: int32 [6, 65536], P(None, ('dom', 'sub')), may hold values from 0 to 1
- neighbours: int32 [6, 65536], P(None, ('dom', 'sub')), may hold values from 0 to 239, as said below
- send_near: int32 [2, 16384], P(None, ('dom', 'sub')), may hold values from 0 to 127
- send_far: int32 [2, 4096], P(None, ('dom', 'sub')), may hold values from 0 to 127
- sub_send: int32 [4096], P(('dom', 'sub')), may hold values from 0 to 127
- partner: int32 [65536], P(('dom', 'sub')), may hold values from 0 to 143, as said below
- pair_send: int32 [8192], P(('dom', 'sub')), may hold values from 0 to 127, as said below
Outputs:
- solution: float32 [64, 8, 65536], P(None, None, ('dom', 'sub'))
- residual: float32 [64, 8, 65536], P(None, None, ('dom', 'sub'))
The draws below stay inside these ranges and needn't reach their ends.
Inputs may be any that keep to these rules, and one draw needn't show every extreme that they name: `neighbours`: values below 128 are the device's own elements; the rest index its 112 received rows in the order of the first step. On each device the partner relation is mutual: local values pair two distinct local elements with each other; each value 128 + q for q below 16 appears exactly once, and the element holding it is entry q of the device's pair_send. `pair_send`: on each device the 16 entries are distinct; slot q pairs with slot q of the device whose sub index differs in the lowest bit.
All inputs are finite; a program needn't handle non-finite values.
Results may differ from the reference program's by a relative error of at most 0.012.
Values may be sent and summed in bfloat16 or wider, within the bound.
No kernel may reach another device: no remote copies, remote signals or barrier semaphores. Data moves between devices by JAX's collectives and lax.ppermute only.
A program may use at most 64 MiB of HBM per device.

```python
import jax
import jax.numpy as jnp

DOF = 64
RHS = 8
NT = 2
NF = 2
SWEEPS = 2
E_DEV = 128
S_NEAR = 32
S_FAR = 8
S_SUB = 8
PAIRS = 16
HALO_ROWS = 112
NE = 65536
N_DOM = 128
N_SUB = 4


def noisy_square(key, leading):
    noise = jax.random.normal(key, (leading, DOF, DOF), jnp.float32)
    return noise


def draw_diag_blocks(key, part):
    noise = noisy_square(key, NT)
    identity = jnp.eye(DOF, dtype=jnp.float32)[None]
    return (2.0 * identity + 0.06 * noise).astype(jnp.bfloat16)


def draw_smoother(key, part):
    noise = noisy_square(key, NT)
    identity = jnp.eye(DOF, dtype=jnp.float32)[None]
    return (0.4 * identity + 0.015 * noise).astype(jnp.bfloat16)


def draw_coarse_inverse(key, part):
    noise = noisy_square(key, 1)[0]
    identity = jnp.eye(DOF, dtype=jnp.float32)
    return (0.25 * identity + 0.01 * noise).astype(jnp.bfloat16)


def draw_neighbours(key, part):
    pick_key, local_key, halo_key = jax.random.split(jax.random.fold_in(key, 5), 3)
    chooser = jax.random.randint(pick_key, (6, NE), 0, 4)
    local_rows = jax.random.randint(local_key, (6, NE), 0, E_DEV)
    halo_rows = E_DEV + jax.random.randint(halo_key, (6, NE), 0, HALO_ROWS)
    result = jnp.where(chooser == 0, halo_rows, local_rows).astype(jnp.int32)
    result = result.at[0, 0].set(E_DEV + HALO_ROWS - 1)
    result = result.at[1, 0].set(0)
    return result


def pairing(key):
    devices = NE // E_DEV
    keys = jax.random.split(jax.random.fold_in(key, 17), devices)
    orders = jax.vmap(lambda single: jax.random.permutation(single, E_DEV))(keys).astype(jnp.int32)
    slots = jnp.arange(E_DEV, dtype=jnp.int32)
    mates = PAIRS + jnp.bitwise_xor(jnp.maximum(slots - PAIRS, 0), 1)
    mates = jnp.where(slots < PAIRS, slots, mates)
    values = jnp.take(orders, mates, axis=1)
    values = jnp.where(slots[None, :] < PAIRS, E_DEV + slots[None, :], values)
    device_rows = jnp.arange(devices, dtype=jnp.int32)[:, None]
    partner = jnp.zeros((devices, E_DEV), jnp.int32).at[device_rows, orders].set(values)
    return (partner.reshape(-1), orders[:, :PAIRS].reshape(-1))


def draw_partner(key, part):
    return pairing(key)[0]


def draw_pair_send(key, part):
    return pairing(key)[1]


def touch_ends(entries, rng, smallest, largest):
    place = [jax.random.randint(jax.random.fold_in(rng, axis), (), 0, length) for axis, length in enumerate(entries.shape)]
    widest = entries.shape.index(max(entries.shape))
    beside = place[:widest] + [(place[widest] + 1) % entries.shape[widest]] + place[widest + 1:]
    return entries.at[tuple(place)].set(smallest).at[tuple(beside)].set(largest)


def steps_of(stream_key, extent, cuts, low, largest):
    level, own = 1.0, jax.random.fold_in(stream_key, 6)
    for dim, blocks in cuts:
        steps = jnp.exp(jax.random.uniform(jax.random.fold_in(own, dim), (blocks,), jnp.float32, low / len(cuts), largest / len(cuts)))
        level = level * jnp.repeat(steps, extent[dim] // blocks).reshape([-1 if axis == dim else 1 for axis in range(len(extent))])
    return level


def normal_values(rng, shape, deviation, bound, cuts=(), kind=jnp.bfloat16):
    entries = deviation * jax.random.normal(rng, shape, jnp.float32)
    if cuts:
        entries = entries * steps_of(rng, shape, cuts, -0.22, 0.18)
    return jnp.clip(entries, -bound, bound).astype(kind)


def setup_inputs(seed: int = 0) -> dict:
    key_list = jax.random.split(jax.random.key(seed), 15)
    rhs = normal_values(key_list[0], (DOF, RHS, NE), 1.0, 6.0, ((2, 512),), jnp.float32)
    guess = normal_values(key_list[1], (DOF, RHS, NE), 0.5, 4.0, ((2, 512),), jnp.float32)
    diag_blocks = draw_diag_blocks(jax.random.fold_in(key_list[14], 71), 0)
    face_blocks = normal_values(key_list[3], (6, NF, DOF, DOF), (6 * DOF) ** -0.5, 0.3125)
    smoother = draw_smoother(jax.random.fold_in(key_list[14], 71), 0)
    coarse_inverse = draw_coarse_inverse(jax.random.fold_in(key_list[14], 71), 0)
    elem_type = touch_ends(jax.random.randint(key_list[6], (NE,), 0, NT), jax.random.fold_in(key_list[6], 1), 0, NT - 1).astype(jnp.int32)
    face_type = touch_ends(jax.random.randint(key_list[7], (6, NE), 0, NF), jax.random.fold_in(key_list[7], 1), 0, NF - 1).astype(jnp.int32)
    neighbours = draw_neighbours(jax.random.fold_in(key_list[14], 71), 0)
    send_near = touch_ends(jax.random.randint(key_list[9], (2, S_NEAR * N_DOM * N_SUB), 0, E_DEV), jax.random.fold_in(key_list[9], 1), 0, E_DEV - 1).astype(jnp.int32)
    send_far = touch_ends(jax.random.randint(key_list[10], (2, S_FAR * N_DOM * N_SUB), 0, E_DEV), jax.random.fold_in(key_list[10], 1), 0, E_DEV - 1).astype(jnp.int32)
    sub_send = touch_ends(jax.random.randint(key_list[11], (S_SUB * N_DOM * N_SUB,), 0, E_DEV), jax.random.fold_in(key_list[11], 1), 0, E_DEV - 1).astype(jnp.int32)
    partner = draw_partner(jax.random.fold_in(key_list[14], 71), 0)
    pair_send = draw_pair_send(jax.random.fold_in(key_list[14], 71), 0)
    return dict(rhs=rhs, guess=guess, diag_blocks=diag_blocks, face_blocks=face_blocks, smoother=smoother, coarse_inverse=coarse_inverse, elem_type=elem_type, face_type=face_type, neighbours=neighbours, send_near=send_near, send_far=send_far, sub_send=sub_send, partner=partner, pair_send=pair_send)


def stack_apply(blocks, field_b, kinds):
    variants = blocks.shape[0]
    node_rows, rhs_width, elements = field_b.shape
    blank = jnp.zeros_like(field_b)
    pieces = [jnp.where(kinds[None, None, :] == variant, field_b, blank) for variant in range(variants)]
    operand = jnp.concatenate(pieces, axis=0).reshape(variants * node_rows, rhs_width * elements)
    wide_blocks = jnp.concatenate([blocks[variant] for variant in range(variants)], axis=1)
    product = jnp.dot(wide_blocks, operand, preferred_element_type=jnp.float32)
    return product.reshape(node_rows, rhs_width, elements)


def list_entry(lists, row_number, width, source_dom, sub_index, slot):
    inside = (source_dom >= 0) & (source_dom < N_DOM)
    source = jnp.clip(source_dom, 0, N_DOM - 1) * N_SUB + sub_index
    position = source * width + jnp.clip(slot, 0, width - 1)
    element = jnp.take(lists[row_number], position)
    return jnp.where(inside, source * E_DEV + element, NE)


def neighbour_global(neighbours, send_near, send_far, sub_send):
    device = (jnp.arange(NE, dtype=jnp.int32) // E_DEV)[None, :]
    dom_index = device // N_SUB
    sub_index = device % N_SUB
    target = neighbours
    start_below = E_DEV
    start_above = start_below + S_NEAR
    start_far_below = start_above + S_NEAR
    start_far_above = start_far_below + S_FAR
    start_sub = start_far_above + S_FAR
    own_rows = device * E_DEV + target
    below = list_entry(send_near, 1, S_NEAR, dom_index - 1, sub_index, target - start_below)
    above = list_entry(send_near, 0, S_NEAR, dom_index + 1, sub_index, target - start_above)
    far_below = list_entry(send_far, 1, S_FAR, dom_index - 2, sub_index, target - start_far_below)
    far_above = list_entry(send_far, 0, S_FAR, dom_index + 2, sub_index, target - start_far_above)
    offset = jnp.maximum(target - start_sub, 0)
    peer_sub = jnp.clip(offset // S_SUB, 0, N_SUB - 1)
    source = dom_index * N_SUB + peer_sub
    side_rows = source * E_DEV + jnp.take(sub_send, source * S_SUB + offset % S_SUB)
    result = jnp.where(target < start_sub, far_above, side_rows)
    result = jnp.where(target < start_far_above, far_below, result)
    result = jnp.where(target < start_far_below, above, result)
    result = jnp.where(target < start_above, below, result)
    result = jnp.where(target < start_below, own_rows, result)
    return result.astype(jnp.int32)


def partner_global(partner, pair_send):
    device = jnp.arange(NE, dtype=jnp.int32) // E_DEV
    source = (device // N_SUB) * N_SUB + jnp.bitwise_xor(device % N_SUB, 1)
    slot = jnp.clip(partner - E_DEV, 0, PAIRS - 1)
    remote = source * E_DEV + jnp.take(pair_send, source * PAIRS + slot)
    return jnp.where(partner < E_DEV, device * E_DEV + partner, remote).astype(jnp.int32)


def apply_global(field_b, index, diag_blocks, face_blocks, elem_type, face_type):
    node_rows, rhs_width, elements = field_b.shape
    padded = jnp.concatenate([field_b, jnp.zeros((node_rows, rhs_width, 1), jnp.bfloat16)], axis=2)
    total = stack_apply(diag_blocks, field_b, elem_type)
    for face_index in range(6):
        beside = jnp.take(padded, index[face_index], axis=2)
        total = total + stack_apply(face_blocks[face_index], beside, face_type[face_index])
    return total


def reference(rhs, guess, diag_blocks, face_blocks, smoother, coarse_inverse, elem_type, face_type, neighbours, send_near, send_far, sub_send, partner, pair_send):
    index = neighbour_global(neighbours, send_near, send_far, sub_send)
    iterate = guess
    for rounds in range(SWEEPS):
        sweep_in = iterate.astype(jnp.bfloat16)
        sweep_res = rhs - apply_global(sweep_in, index, diag_blocks, face_blocks, elem_type, face_type)
        iterate = iterate + stack_apply(smoother, sweep_res.astype(jnp.bfloat16), elem_type)
    final_in = iterate.astype(jnp.bfloat16)
    residual = rhs - apply_global(final_in, index, diag_blocks, face_blocks, elem_type, face_type)
    mates = partner_global(partner, pair_send)
    coarse = residual + jnp.take(residual, mates, axis=2)
    node_rows, rhs_width, elements = coarse.shape
    coarse_b = coarse.astype(jnp.bfloat16).reshape(node_rows, rhs_width * elements)
    update = jnp.dot(coarse_inverse, coarse_b, preferred_element_type=jnp.float32)
    solution = iterate + update.reshape(node_rows, rhs_width, elements)
    return (solution, residual)
```

```python
import functools

import jax
import jax.numpy as jnp
from jax import lax
from jax.experimental import pallas as pl
from jax.experimental.pallas import tpu as pltpu
from jax.sharding import PartitionSpec as P

SWEEPS = 2
DOF = 64
RHS = 8
E = 128
FACES = 6
ROWS = DOF * RHS
BF = jnp.bfloat16
F32 = jnp.float32

SPLIT = (32, 32, 16, 16, 32)
HALO = sum(SPLIT)
PAIRS = 16


def swap(array, axis, pairs):
    count = lax.axis_size(axis)
    route = []
    for low, high in pairs:
        if high < count:
            route += [(low, high), (high, low)]
    return lax.ppermute(array, axis, route)


def spec():
    return pl.BlockSpec(memory_space=pltpu.VMEM)


def call(kernel, outs, *args, flops=0, scalars=0):
    specs = [pl.BlockSpec(memory_space=pltpu.SMEM)] * scalars
    specs += [spec()] * (len(args) - scalars)
    moved = sum(a.size * a.dtype.itemsize for a in args)
    return pl.pallas_call(
        kernel,
        out_shape=[jax.ShapeDtypeStruct(s, d) for s, d in outs],
        in_specs=specs,
        out_specs=[spec()] * len(outs),
        cost_estimate=pl.CostEstimate(flops=flops, bytes_accessed=moved, transcendentals=0),
        compiler_params=pltpu.CompilerParams(vmem_limit_bytes=32 << 20),
    )(*args)


def iota(shape, dim):
    return lax.broadcasted_iota(jnp.int32, shape, dim)


def column(row):
    count = row.shape[1]
    wide = jnp.broadcast_to(row.astype(F32), (count, count))
    kept = jnp.where(iota((count, count), 0) == iota((count, count), 1), wide, 0.0)
    return jnp.sum(kept, axis=1, keepdims=True).astype(jnp.int32)


def picker(row):
    count = row.shape[1]
    return jnp.where(iota((count, E), 1) == column(row), 1.0, 0.0).astype(BF)


def send(choice, field, refs):
    rows = lax.dot_general(choice, field, (((1,), (1,)), ((), ())), preferred_element_type=F32).astype(BF)
    start = 0
    for ref in refs:
        ref[...] = rows[start : start + ref.shape[0]]
        start += ref.shape[0]


def pack_kernel(odd_ref, guess, near, far, sub, pair, field_ref, choice_ref, *messages):
    odd_core = odd_ref[0] == 1
    odd_chip = odd_ref[1] == 1
    for r in range(RHS):
        field_ref[r * DOF : (r + 1) * DOF, :] = guess[pl.ds(r, DOF, stride=RHS), :].astype(BF)
    lower, higher = near[0:1, :], near[1:2, :]
    far_lower, far_higher = far[0:1, :], far[1:2, :]
    blank = jnp.zeros((8, E), BF)
    side = picker(sub[...])
    choice = jnp.concatenate(
        [
            picker(jnp.where(odd_core, lower, higher)),
            picker(jnp.where(odd_core, higher, lower)),
            picker(jnp.where(odd_chip, far_lower, far_higher)),
            blank,
            picker(jnp.where(odd_chip, far_higher, far_lower)),
            blank,
            side,
            side,
            side,
            side,
            picker(pair[...]),
        ],
        axis=0,
    )
    choice_ref[...] = choice
    send(choice[:HALO], field_ref[...], messages)


def prep_kernel(odd_ref, diag, face, smooth, elem_type, face_type, neighbours, partner, pick_ref, mask_ref, wide_ref, smooth_ref, mate_ref):
    odd_core = odd_ref[0]
    odd_chip = odd_ref[1]
    for d in range(FACES):
        k = neighbours[d : d + 1, :]
        below = jnp.where(odd_core == 1, 0, 32)
        above = jnp.where(odd_core == 1, 0, -32)
        far_below = jnp.where(odd_chip == 1, 0, 16)
        far_above = jnp.where(odd_chip == 1, 8, -8)
        shift = jnp.where(k < 208, far_above, 16)
        shift = jnp.where(k < 200, far_below, shift)
        shift = jnp.where(k < 192, above, shift)
        shift = jnp.where(k < 160, below, shift)
        place = k + jnp.where(k < 128, 0, shift)
        hot = jnp.where(iota((E + HALO, E), 0) == place, 1.0, 0.0)
        pick_ref[:, d * E : (d + 1) * E] = hot.astype(BF)
    for d in range(FACES + 1):
        kinds = elem_type[...] if d == 0 else face_type[d - 1 : d, :]
        for t in range(2):
            mask = jnp.where(jnp.broadcast_to(kinds, (16, E)) == t, 1.0, 0.0)
            mask_ref[2 * d + t] = mask.astype(BF)
        pair = (diag[0], diag[1]) if d == 0 else (face[d - 1, 0], face[d - 1, 1])
        wide_ref[:, d * 2 * DOF : (d + 1) * 2 * DOF] = jnp.concatenate(pair, axis=1)
    smooth_ref[...] = jnp.concatenate([smooth[0], smooth[1]], axis=1)
    mate_ref[...] = jnp.where(iota((E + PAIRS, E), 0) == partner[...], 1.0, 0.0).astype(BF)


def masked(block, mask):
    full = jnp.concatenate([mask] * (DOF // 16), axis=0)
    return block * full


def residual_of(field_ref, halo, pick, masks, wide, rhs, take):
    near = jnp.concatenate([ref[...] for ref in halo], axis=0)
    field = field_ref[...]
    beside = jnp.dot(field, pick[:E, :], preferred_element_type=F32)
    beside = beside + lax.dot_general(near, pick[E:, :], (((0,), (0,)), ((), ())), preferred_element_type=F32)
    beside = beside.astype(BF)
    for r in range(0, RHS, 2):
        halves = []
        for s in (r, r + 1):
            stack = []
            for d in range(FACES + 1):
                block = field[s * DOF : (s + 1) * DOF, :] if d == 0 else beside[s * DOF : (s + 1) * DOF, (d - 1) * E : d * E]
                stack += [masked(block, masks[2 * d]), masked(block, masks[2 * d + 1])]
            halves.append(jnp.concatenate(stack, axis=0))
        product = jnp.dot(wide[...], jnp.concatenate(halves, axis=1), preferred_element_type=F32)
        right = jnp.concatenate([rhs[pl.ds(s, DOF, stride=RHS), :] for s in (r, r + 1)], axis=1)
        take(r, right - product)


def sweep_kernel(first, field_ref, n1, n2, f1, f2, side, pick, masks, wide, smooth, rhs, before, choice, after, next_field, *messages):
    def take(r, residual):
        rounded = residual.astype(BF)
        halves = []
        for i in range(2):
            block = rounded[:, i * E : (i + 1) * E]
            halves.append(jnp.concatenate([masked(block, masks[0]), masked(block, masks[1])], axis=0))
        change = jnp.dot(smooth[...], jnp.concatenate(halves, axis=1), preferred_element_type=F32)
        for i in range(2):
            s = r + i
            rows = slice(s * DOF, (s + 1) * DOF)
            old = before[pl.ds(s, DOF, stride=RHS), :] if first else before[rows, :]
            new = old + change[:, i * E : (i + 1) * E]
            after[rows, :] = new
            next_field[rows, :] = new.astype(BF)

    residual_of(field_ref, (n1, n2, f1, f2, side), pick, masks, wide, rhs, take)
    send(choice[:HALO, :], next_field[...], messages)


def residual_kernel(field_ref, n1, n2, f1, f2, side, pick, masks, wide, rhs, choice, residual_ref, rounded_ref, rest_ref, message):
    def take(r, residual):
        for i in range(2):
            s = r + i
            part = residual[:, i * E : (i + 1) * E]
            residual_ref[pl.ds(s, DOF, stride=RHS), :] = part
            rounded = part.astype(BF)
            rounded_ref[s * DOF : (s + 1) * DOF, :] = rounded
            rest_ref[s * DOF : (s + 1) * DOF, :] = (part - rounded.astype(F32)).astype(BF)

    residual_of(field_ref, (n1, n2, f1, f2, side), pick, masks, wide, rhs, take)
    send(choice[HALO:, :], rounded_ref[...], (message,))


def coarse_kernel(residual_ref, rounded_ref, rest_ref, incoming, mate, inverse, iterate, solution_ref):
    local = mate[:E, :]
    mates = jnp.dot(rounded_ref[...], local, preferred_element_type=F32)
    mates = mates + jnp.dot(rest_ref[...], local, preferred_element_type=F32)
    mates = mates + lax.dot_general(incoming[...], mate[E:, :], (((0,), (0,)), ((), ())), preferred_element_type=F32)
    for r in range(0, RHS, 2):
        halves = []
        for s in (r, r + 1):
            coarse = residual_ref[pl.ds(s, DOF, stride=RHS), :] + mates[s * DOF : (s + 1) * DOF, :]
            halves.append(coarse.astype(BF))
        update = jnp.dot(inverse[...], jnp.concatenate(halves, axis=1), preferred_element_type=F32)
        for i in range(2):
            s = r + i
            solution_ref[pl.ds(s, DOF, stride=RHS), :] = iterate[s * DOF : (s + 1) * DOF, :] + update[:, i * E : (i + 1) * E]


def body(
    rhs,
    guess,
    diag_blocks,
    face_blocks,
    smoother,
    coarse_inverse,
    elem_type,
    face_type,
    neighbours,
    send_near,
    send_far,
    sub_send,
    partner,
    pair_send,
):
    a = lax.axis_index("dom")
    odd = jnp.stack([a % 2, (a // 2) % 2]).astype(jnp.int32)
    doms = lax.axis_size("dom")
    rhs = rhs.reshape(ROWS, E)
    guess = guess.reshape(ROWS, E)
    inside = [(i, i + 1) for i in range(0, doms, 2)]
    across = [(i + 1, i + 2) for i in range(0, doms, 2)]
    far_one = [(i + j, i + j + 2) for i in range(0, doms, 4) for j in range(2)]
    far_two = [(i + j + 2, i + j + 4) for i in range(0, doms, 4) for j in range(2)]

    def exchange(messages):
        n1, n2, f1, f2, side = messages
        return (
            swap(n1, "dom", inside),
            swap(n2, "dom", across),
            swap(f1, "dom", far_one),
            swap(f2, "dom", far_two),
            lax.all_to_all(side, "sub", 0, 0, tiled=True),
        )

    message_outs = [((n, ROWS), BF) for n in SPLIT]
    field, choice, *messages = call(
        pack_kernel,
        [((ROWS, E), BF), ((HALO + PAIRS, E), BF)] + message_outs,
        odd,
        guess,
        send_near,
        send_far,
        sub_send.reshape(1, -1),
        pair_send.reshape(1, -1),
        flops=2 * HALO * E * ROWS,
        scalars=1,
    )
    halo = exchange(messages)
    pick, masks, wide, smooth, mate = call(
        prep_kernel,
        [
            ((E + HALO, FACES * E), BF),
            ((2 * FACES + 2, 16, E), BF),
            ((DOF, 2 * DOF * (FACES + 1)), BF),
            ((DOF, 2 * DOF), BF),
            ((E + PAIRS, E), BF),
        ],
        odd,
        diag_blocks,
        face_blocks,
        smoother,
        elem_type.reshape(1, -1),
        face_type,
        neighbours,
        partner.reshape(1, -1),
        flops=1000000,
        scalars=1,
    )
    work = 2 * ROWS * (E + HALO) * FACES * E + 2 * DOF * 14 * DOF * RHS * E
    iterate = guess
    for rounds in range(SWEEPS):
        iterate, field, *messages = call(
            functools.partial(sweep_kernel, rounds == 0),
            [((ROWS, E), F32), ((ROWS, E), BF)] + message_outs,
            field,
            *halo,
            pick,
            masks,
            wide,
            smooth,
            rhs,
            iterate,
            choice,
            flops=work,
        )
        halo = exchange(messages)
    residual, rounded, rest, message = call(
        residual_kernel,
        [((ROWS, E), F32), ((ROWS, E), BF), ((ROWS, E), BF), ((PAIRS, ROWS), BF)],
        field,
        *halo,
        pick,
        masks,
        wide,
        rhs,
        choice,
        flops=work,
    )
    subs = lax.axis_size("sub")
    incoming = swap(message, "sub", [(i, i + 1) for i in range(0, subs, 2)])
    (solved,) = call(
        coarse_kernel,
        [((ROWS, E), F32)],
        residual,
        rounded,
        rest,
        incoming,
        mate,
        coarse_inverse,
        iterate,
        flops=work // 4,
    )
    shape = (DOF, RHS, E)
    return (solved.reshape(shape), residual.reshape(shape))


def solution(mesh):
    block = P(None, None, ("dom", "sub"))
    flat = P(("dom", "sub"))
    listed = P(None, ("dom", "sub"))
    in_specs = (block, block, P(), P(), P(), P(), flat, listed, listed, listed, listed, flat, flat, flat)
    return jax.shard_map(body, mesh=mesh, in_specs=in_specs, out_specs=(block, block), check_vma=False)
```

```python
import functools

import jax
import jax.numpy as jnp
from jax import lax
from jax.experimental import pallas as pl
from jax.experimental.pallas import tpu as pltpu
from jax.sharding import PartitionSpec as P

SWEEPS = 2
DOF = 64
RHS = 8
E = 128
FACES = 6
ROWS = DOF * RHS
BF = jnp.bfloat16
F32 = jnp.float32

SPLIT = (32, 32, 16, 16, 32)
SENT = (32, 48, 16, 48, 32)
HALO = sum(SPLIT)
PAIRS = 16


def swap(array, axis, pairs):
    count = lax.axis_size(axis)
    route = []
    for low, high in pairs:
        if high < count:
            route += [(low, high), (high, low)]
    return lax.ppermute(array, axis, route)


def spec():
    return pl.BlockSpec(memory_space=pltpu.VMEM)


def call(kernel, outs, *args, flops=0, scalars=0):
    specs = [pl.BlockSpec(memory_space=pltpu.SMEM)] * scalars
    specs += [spec()] * (len(args) - scalars)
    moved = sum(a.size * a.dtype.itemsize for a in args)
    return pl.pallas_call(
        kernel,
        out_shape=[jax.ShapeDtypeStruct(s, d) for s, d in outs],
        in_specs=specs,
        out_specs=[spec()] * len(outs),
        cost_estimate=pl.CostEstimate(flops=flops, bytes_accessed=moved, transcendentals=0),
        compiler_params=pltpu.CompilerParams(vmem_limit_bytes=32 << 20),
    )(*args)


def iota(shape, dim):
    return lax.broadcasted_iota(jnp.int32, shape, dim)


def column(row):
    count = row.shape[1]
    wide = jnp.broadcast_to(row.astype(F32), (count, count))
    kept = jnp.where(iota((count, count), 0) == iota((count, count), 1), wide, 0.0)
    return jnp.sum(kept, axis=1, keepdims=True).astype(jnp.int32)


def picker(row):
    count = row.shape[1]
    return jnp.where(iota((count, E), 1) == column(row), 1.0, 0.0).astype(BF)


def send(choice, field, refs):
    rows = lax.dot_general(choice, field, (((1,), (1,)), ((), ())), preferred_element_type=F32).astype(BF)
    start = 0
    for ref, used in refs:
        ref[:used] = rows[start : start + used]
        if ref.shape[0] > used:
            ref[used:] = jnp.zeros((ref.shape[0] - used, ROWS), BF)
        start += used


def pack_kernel(odd_ref, guess, near, far, sub, field_ref, choice_ref, *messages):
    odd_core = odd_ref[0] == 1
    odd_chip = odd_ref[1] == 1
    lower, higher = near[0:1, :], near[1:2, :]
    far_lower, far_higher = far[0:1, :], far[1:2, :]
    blank = jnp.zeros((8, E), BF)
    side = picker(sub[...])
    choice = jnp.concatenate(
        [
            picker(jnp.where(odd_core, lower, higher)),
            picker(jnp.where(odd_core, higher, lower)),
            picker(jnp.where(odd_chip, far_lower, far_higher)),
            blank,
            picker(jnp.where(odd_chip, far_higher, far_lower)),
            blank,
            side,
            side,
            side,
            side,
        ],
        axis=0,
    )
    choice_ref[...] = choice
    for r in range(RHS):
        field_ref[r * DOF : (r + 1) * DOF, :] = guess[pl.ds(r, DOF, stride=RHS), :].astype(BF)
    send(choice, field_ref[...], zip(messages, SPLIT))


def prep_kernel(odd_ref, diag, face, smooth, neighbours, face_type, elem_type, pick_ref, mask_ref, wide_ref, smooth_ref):
    odd_core = odd_ref[0]
    odd_chip = odd_ref[1]
    for d in range(FACES):
        k = neighbours[d : d + 1, :]
        below = jnp.where(odd_core == 1, 0, 32)
        above = jnp.where(odd_core == 1, 0, -32)
        far_below = jnp.where(odd_chip == 1, 0, 16)
        far_above = jnp.where(odd_chip == 1, 8, -8)
        shift = jnp.where(k < 208, far_above, 16)
        shift = jnp.where(k < 200, far_below, shift)
        shift = jnp.where(k < 192, above, shift)
        shift = jnp.where(k < 160, below, shift)
        place = k + jnp.where(k < 128, 0, shift)
        hot = jnp.where(iota((E + HALO, E), 0) == place, 1.0, 0.0)
        pick_ref[:, d * E : (d + 1) * E] = hot.astype(BF)
    for d in range(FACES + 1):
        kinds = elem_type[...] if d == 0 else face_type[d - 1 : d, :]
        for t in range(2):
            mask = jnp.where(jnp.broadcast_to(kinds, (16, E)) == t, 1.0, 0.0)
            mask_ref[2 * d + t] = mask.astype(BF)
        both = (diag[0], diag[1]) if d == 0 else (face[d - 1, 0], face[d - 1, 1])
        wide_ref[:, d * 2 * DOF : (d + 1) * 2 * DOF] = jnp.concatenate(both, axis=1)
    smooth_ref[...] = jnp.concatenate([smooth[0], smooth[1]], axis=1)


def masked(block, mask):
    full = jnp.concatenate([mask] * (DOF // 16), axis=0)
    return block * full


def residual_of(field_ref, halo, pick, masks, wide, rhs, take):
    near = jnp.concatenate([ref[:used] for ref, used in zip(halo, SPLIT)], axis=0)
    field = field_ref[...]
    extended = jnp.concatenate([field, near.T], axis=1)
    beside = jnp.dot(extended, pick[...], preferred_element_type=F32).astype(BF)
    for r in range(0, RHS, 2):
        halves = []
        for s in (r, r + 1):
            stack = []
            for d in range(FACES + 1):
                block = field[s * DOF : (s + 1) * DOF, :] if d == 0 else beside[s * DOF : (s + 1) * DOF, (d - 1) * E : d * E]
                stack += [masked(block, masks[2 * d]), masked(block, masks[2 * d + 1])]
            halves.append(jnp.concatenate(stack, axis=0))
        product = jnp.dot(wide[...], jnp.concatenate(halves, axis=1), preferred_element_type=F32)
        right = jnp.concatenate([rhs[pl.ds(s, DOF, stride=RHS), :] for s in (r, r + 1)], axis=1)
        take(r, right - product)


def sweep_kernel(first, field_ref, f2, n2, f1, n1, side, pick, masks, wide, smooth, rhs, before, choice, after, next_field, *messages):
    def take(r, residual):
        rounded = residual.astype(BF)
        halves = []
        for i in range(2):
            block = rounded[:, i * E : (i + 1) * E]
            halves.append(jnp.concatenate([masked(block, masks[0]), masked(block, masks[1])], axis=0))
        change = jnp.dot(smooth[...], jnp.concatenate(halves, axis=1), preferred_element_type=F32)
        for i in range(2):
            s = r + i
            rows = slice(s * DOF, (s + 1) * DOF)
            old = before[pl.ds(s, DOF, stride=RHS), :] if first else before[rows, :]
            new = old + change[:, i * E : (i + 1) * E]
            after[rows, :] = new
            next_field[rows, :] = new.astype(BF)

    residual_of(field_ref, (n1, n2, f1, f2, side), pick, masks, wide, rhs, take)
    send(choice[...], next_field[...], zip(messages, SPLIT))


def residual_kernel(field_ref, f2, n2, f1, n1, side, pick, masks, wide, rhs, pair, residual_ref, rounded_ref, message):
    def take(r, residual):
        for i in range(2):
            rows = slice((r + i) * DOF, (r + i + 1) * DOF)
            part = residual[:, i * E : (i + 1) * E]
            residual_ref[rows, :] = part
            rounded_ref[rows, :] = part.astype(BF)

    residual_of(field_ref, (n1, n2, f1, f2, side), pick, masks, wide, rhs, take)
    send(picker(pair[...]), rounded_ref[...], [(message, PAIRS)])


def mate_picker(partner, first, count):
    return jnp.where(iota((count, E), 0) + first == partner, 1.0, 0.0).astype(BF)


def local_kernel(residual_ref, rounded_ref, partner, out_ref, half_ref):
    rest = (residual_ref[...] - rounded_ref[...].astype(F32)).astype(BF)
    local = mate_picker(partner[...], 0, E)
    mates = jnp.dot(rounded_ref[...], local, preferred_element_type=F32)
    mates = mates + jnp.dot(rest, local, preferred_element_type=F32)
    half_ref[...] = residual_ref[...] + mates
    for r in range(RHS):
        out_ref[pl.ds(r, DOF, stride=RHS), :] = residual_ref[r * DOF : (r + 1) * DOF, :]


def coarse_kernel(half_ref, incoming, partner, inverse, iterate, solution_ref):
    mates = lax.dot_general(incoming[...], mate_picker(partner[...], E, PAIRS), (((0,), (0,)), ((), ())), preferred_element_type=F32)
    coarse = (half_ref[...] + mates).astype(BF)
    for r in range(0, RHS, 2):
        pair = jnp.concatenate([coarse[s * DOF : (s + 1) * DOF, :] for s in (r, r + 1)], axis=1)
        update = jnp.dot(inverse[...], pair, preferred_element_type=F32)
        for i in range(2):
            s = r + i
            solution_ref[pl.ds(s, DOF, stride=RHS), :] = iterate[s * DOF : (s + 1) * DOF, :] + update[:, i * E : (i + 1) * E]


def body(
    rhs,
    guess,
    diag_blocks,
    face_blocks,
    smoother,
    coarse_inverse,
    elem_type,
    face_type,
    neighbours,
    send_near,
    send_far,
    sub_send,
    partner,
    pair_send,
):
    a = lax.axis_index("dom")
    odd = jnp.stack([a % 2, (a // 2) % 2]).astype(jnp.int32)
    doms = lax.axis_size("dom")
    rhs = rhs.reshape(ROWS, E)
    guess = guess.reshape(ROWS, E)
    inside = [(i, i + 1) for i in range(0, doms, 2)]
    across = [(i + 1, i + 2) for i in range(0, doms, 2)]
    far_one = [(i + j, i + j + 2) for i in range(0, doms, 4) for j in range(2)]
    far_two = [(i + j + 2, i + j + 4) for i in range(0, doms, 4) for j in range(2)]

    def exchange(messages):
        n1, n2, f1, f2, side = messages
        f2 = swap(f2, "dom", far_two)
        n2 = swap(n2, "dom", across)
        f1 = swap(f1, "dom", far_one)
        n1 = swap(n1, "dom", inside)
        side = lax.all_to_all(side, "sub", 0, 0, tiled=True)
        return f2, n2, f1, n1, side

    message_outs = [((n, ROWS), BF) for n in SENT]
    field, choice, *messages = call(
        pack_kernel,
        [((ROWS, E), BF), ((HALO, E), BF)] + message_outs,
        odd,
        guess,
        send_near,
        send_far,
        sub_send.reshape(1, -1),
        flops=2 * HALO * E * ROWS,
        scalars=1,
    )
    halo = exchange(messages)
    pick, masks, wide, smooth = call(
        prep_kernel,
        [
            ((E + HALO, FACES * E), BF),
            ((2 * FACES + 2, 16, E), BF),
            ((DOF, 2 * DOF * (FACES + 1)), BF),
            ((DOF, 2 * DOF), BF),
        ],
        odd,
        diag_blocks,
        face_blocks,
        smoother,
        neighbours,
        face_type,
        elem_type.reshape(1, -1),
        flops=1000000,
        scalars=1,
    )
    work = 2 * ROWS * (E + HALO) * FACES * E + 2 * DOF * 14 * DOF * RHS * E
    iterate = guess
    for rounds in range(SWEEPS):
        iterate, field, *messages = call(
            functools.partial(sweep_kernel, rounds == 0),
            [((ROWS, E), F32), ((ROWS, E), BF)] + message_outs,
            field,
            *halo,
            pick,
            masks,
            wide,
            smooth,
            rhs,
            iterate,
            choice,
            flops=work,
        )
        halo = exchange(messages)
    residual, rounded, message = call(
        residual_kernel,
        [((ROWS, E), F32), ((ROWS, E), BF), ((PAIRS, ROWS), BF)],
        field,
        *halo,
        pick,
        masks,
        wide,
        rhs,
        pair_send.reshape(1, -1),
        flops=work,
    )
    subs = lax.axis_size("sub")
    incoming = swap(message, "sub", [(i, i + 1) for i in range(0, subs, 2)])
    residual, half = call(
        local_kernel,
        [((ROWS, E), F32), ((ROWS, E), F32)],
        residual,
        rounded,
        partner.reshape(1, -1),
        flops=work // 4,
    )
    (solved,) = call(
        coarse_kernel,
        [((ROWS, E), F32)],
        half,
        incoming,
        partner.reshape(1, -1),
        coarse_inverse,
        iterate,
        flops=work // 4,
    )
    shape = (DOF, RHS, E)
    return (solved.reshape(shape), residual.reshape(shape))


def solution(mesh):
    block = P(None, None, ("dom", "sub"))
    flat = P(("dom", "sub"))
    listed = P(None, ("dom", "sub"))
    in_specs = (block, block, P(), P(), P(), P(), flat, listed, listed, listed, listed, flat, flat, flat)
    return jax.shard_map(body, mesh=mesh, in_specs=in_specs, out_specs=(block, block), check_vma=False)
```

```python
import jax
import jax.numpy as jnp
from jax import lax
from jax.experimental import pallas as pl
from jax.experimental.pallas import tpu as pltpu
from jax.sharding import PartitionSpec as P

SWEEPS = 2
DOF = 64
RHS = 8
E = 128
CHIP = 2 * E
FACES = 6
ROWS = DOF * RHS
NEAR = 32
FAR = 8
SUB = 8
PAIRS = 16
CROSS = NEAR + 2 * FAR
SIDE = 4 * 2 * SUB
KEPT = CHIP + 2 * CROSS + SIDE
INTS = 32
BF = jnp.bfloat16
F32 = jnp.float32


def swap(array, axis, pairs):
    count = lax.axis_size(axis)
    route = []
    for low, high in pairs:
        if high < count:
            route += [(low, high), (high, low)]
    return lax.ppermute(array, axis, route)


def spec():
    return pl.BlockSpec(memory_space=pltpu.VMEM)


def call(kernel, outs, *args, flops=0, scalars=0, remote=0, scratch=(), vmem=16):
    specs = [pl.BlockSpec(memory_space=pltpu.SMEM)] * scalars
    specs += [pl.BlockSpec(memory_space=pl.ANY)] * remote
    specs += [spec()] * (len(args) - scalars - remote)
    moved = sum(a.size * a.dtype.itemsize for a in args)
    return pl.pallas_call(
        kernel,
        out_shape=[jax.ShapeDtypeStruct(s, d) for s, d in outs],
        in_specs=specs,
        out_specs=[spec()] * len(outs),
        scratch_shapes=scratch,
        cost_estimate=pl.CostEstimate(flops=flops, bytes_accessed=moved, transcendentals=0),
        compiler_params=pltpu.CompilerParams(vmem_limit_bytes=vmem << 20),
    )(*args)


def iota(shape, dim):
    return lax.broadcasted_iota(jnp.int32, shape, dim)


def half(core):
    return pl.ds(pl.multiple_of(core * E, E), E)


def column(row):
    count = row.shape[1]
    wide = jnp.broadcast_to(row.astype(F32), (count, count))
    kept = jnp.where(iota((count, count), 0) == iota((count, count), 1), wide, 0.0)
    return jnp.sum(kept, axis=1, keepdims=True).astype(jnp.int32)


def picker(row, width):
    count = row.shape[1]
    return jnp.where(iota((count, width), 1) == column(row), 1.0, 0.0).astype(BF)


def send(choice, field, refs):
    rows = lax.dot_general(choice, field, (((1,), (1,)), ((), ())), preferred_element_type=F32).astype(BF)
    start = 0
    for ref, used in refs:
        ref[:used] = rows[start : start + used]
        if ref.shape[0] > used:
            ref[used:] = jnp.zeros((ref.shape[0] - used, ROWS), BF)
        start += used


def first_kernel(*refs):
    sources, message, targets, ints, arrived = refs[:8], refs[8], refs[9:17], refs[17], refs[18]
    copies = [pltpu.make_async_copy(a, b, arrived.at[i]) for i, (a, b) in enumerate(zip(sources, targets))]
    for copy in copies:
        copy.start()
    near, far, sub, elem_type, face_type, neighbours, guess, rhs = targets
    for copy in copies[:6]:
        copy.wait()
    ints[...] = jnp.zeros((INTS, E), F32)
    ints[0:6, :] = neighbours[...].astype(F32)
    ints[8:14, :] = face_type[...].astype(F32)
    ints[14:15, :] = elem_type[...].astype(F32)
    ints[16:18, :NEAR] = near[...].astype(F32)
    ints[18:20, :FAR] = far[...].astype(F32)
    ints[20:21, :SUB] = sub[...].astype(F32)
    message[2 * ROWS :, :] = ints[...].astype(BF)
    for i, field in enumerate((guess, rhs)):
        copies[6 + i].wait()
        for r in range(RHS):
            start = i * ROWS + r * DOF
            message[start : start + DOF, :] = field[pl.ds(r, DOF, stride=RHS), :].astype(BF)


def pack_kernel(place_ref, mine, other, field_ref, ints_ref, choice_ref, *messages):
    core = place_ref[0]
    odd = place_ref[1] == 1
    field_ref[:, half(core)] = mine[:ROWS, :]
    field_ref[:, half(1 - core)] = other[:ROWS, :]
    ints_ref[core] = mine[2 * ROWS :, :].astype(F32).astype(jnp.int32)
    ints_ref[1 - core] = other[2 * ROWS :, :].astype(F32).astype(jnp.int32)
    low, high = ints_ref[0], ints_ref[1]

    def chosen(near, one, two):
        return picker(near, CHIP), jnp.concatenate([picker(one, CHIP), picker(two + E, CHIP)], axis=0)

    up = (high[17:18, :NEAR] + E, low[19:20, :FAR], high[19:20, :FAR])
    down = (low[16:17, :NEAR], low[18:19, :FAR], high[18:19, :FAR])
    to_one = [jnp.where(odd, d, u) for u, d in zip(up, down)]
    to_two = [jnp.where(odd, u, d) for u, d in zip(up, down)]
    side = jnp.concatenate([picker(low[20:21, :SUB], CHIP), picker(high[20:21, :SUB] + E, CHIP)], axis=0)
    choice = jnp.concatenate([*chosen(*to_one), *chosen(*to_two), side, side, side, side], axis=0)
    choice_ref[...] = choice
    send(choice, field_ref[...], zip(messages, (CROSS, CROSS, SIDE)))


def prep_kernel(place_ref, diag, face, smooth, ints, other, rhs, pick_ref, mask_ref, wide_ref, smooth_ref, rhs_ref):
    core = place_ref[0]
    odd = place_ref[1] == 1
    below = jnp.where(odd, CHIP, CHIP + CROSS)
    above = jnp.where(odd, CHIP + CROSS, CHIP)
    for c in range(2):
        mine, near = ints[c], ints[1 - c]
        listed = near[16:17, :NEAR] if c == 0 else near[17:18, :NEAR]
        inner = jnp.where(iota((E, NEAR), 0) == listed, 1.0, 0.0).astype(BF)
        for d in range(FACES):
            k = mine[d : d + 1, :]
            m = k - 208
            place = CHIP + 2 * CROSS + (m >> 3) * 2 * SUB + c * SUB + (m & 7)
            place = jnp.where(k < 208, above + NEAR + c * FAR + k - 200, place)
            place = jnp.where(k < 200, below + NEAR + c * FAR + k - 192, place)
            place = jnp.where(k < 192, -1 if c == 0 else above + k - 160, place)
            place = jnp.where(k < 160, below + k - 128 if c == 0 else -1, place)
            place = jnp.where(k < E, k + c * E, place)
            lanes = slice(d * CHIP + c * E, d * CHIP + (c + 1) * E)
            hot = jnp.where(iota((KEPT, E), 0) == place, 1.0, 0.0)
            slot = jnp.where(iota((NEAR, E), 0) + (160 if c == 0 else 128) == k, 1.0, 0.0).astype(BF)
            within = jnp.dot(inner, slot, preferred_element_type=F32)
            start = (1 - c) * E
            if start:
                pick_ref[:start, lanes] = hot[:start].astype(BF)
            pick_ref[start : start + E, lanes] = (hot[start : start + E] + within).astype(BF)
            pick_ref[start + E :, lanes] = hot[start + E :].astype(BF)
        for d in range(FACES + 1):
            kinds = mine[14:15, :] if d == 0 else mine[7 + d : 8 + d, :]
            for t in range(2):
                mask = jnp.where(jnp.broadcast_to(kinds, (16, E)) == t, 1.0, 0.0)
                mask_ref[2 * d + t, :, c * E : (c + 1) * E] = mask.astype(BF)
    for d in range(FACES + 1):
        both = (diag[0], diag[1]) if d == 0 else (face[d - 1, 0], face[d - 1, 1])
        wide_ref[:, d * 2 * DOF : (d + 1) * 2 * DOF] = jnp.concatenate(both, axis=1)
    smooth_ref[...] = jnp.concatenate([smooth[0], smooth[1]], axis=1)
    for r in range(RHS):
        rows = slice(r * DOF, (r + 1) * DOF)
        rhs_ref[rows, half(core)] = rhs[pl.ds(r, DOF, stride=RHS), :]
    rhs_ref[:, half(1 - core)] = other[ROWS : 2 * ROWS, :].astype(F32)


def masked(block, mask):
    return block * jnp.concatenate([mask] * (DOF // 16), axis=0)


def extend(field_ref, halo):
    near = jnp.concatenate([ref[:used] for ref, used in zip(halo, (CROSS, CROSS, SIDE))], axis=0)
    return jnp.concatenate([field_ref[...], near.T], axis=1)


def sweep_kernel(place_ref, field_ref, two, one, side, pick, masks, wide, smooth, rhs, choice, *refs):
    core = place_ref[0]
    before, (after, next_field, *messages) = refs[:-5], refs[-5:]
    if len(before) == 2:
        guess, other = before
        for r in range(RHS):
            after[r * DOF : (r + 1) * DOF, half(core)] = guess[pl.ds(r, DOF, stride=RHS), :]
        after[:, half(1 - core)] = other[:ROWS, :].astype(F32)
        before = after
    else:
        (before,) = before
    beside = jnp.dot(extend(field_ref, (one, two, side)), pick[...], preferred_element_type=F32).astype(BF)
    for r in range(RHS):
        rows = slice(r * DOF, (r + 1) * DOF)
        stack = []
        for d in range(FACES + 1):
            block = field_ref[rows, :] if d == 0 else beside[rows, (d - 1) * CHIP : d * CHIP]
            stack += [masked(block, masks[2 * d]), masked(block, masks[2 * d + 1])]
        product = jnp.dot(wide[...], jnp.concatenate(stack, axis=0), preferred_element_type=F32)
        rounded = (rhs[rows, :] - product).astype(BF)
        both = jnp.concatenate([masked(rounded, masks[0]), masked(rounded, masks[1])], axis=0)
        new = before[rows, :] + jnp.dot(smooth[...], both, preferred_element_type=F32)
        after[rows, :] = new
        next_field[rows, :] = new.astype(BF)
    send(choice[...], next_field[...], zip(messages, (CROSS, CROSS, SIDE)))


def residual_kernel(place_ref, field_ref, two, one, side, pick, masks, wide, rhs, pair, residual_ref, rounded_ref, message):
    core = place_ref[0]
    own = half(core)
    extended = extend(field_ref, (one, two, side))
    beside = []
    for d in range(FACES):
        columns = pick[:, pl.ds(pl.multiple_of(d * CHIP + core * E, E), E)]
        beside.append(columns)
    beside = jnp.dot(extended, jnp.concatenate(beside, axis=1), preferred_element_type=F32).astype(BF)
    field = field_ref[:, own]
    kinds = [masks[i, :, own] for i in range(2 * FACES + 2)]
    for r in range(0, RHS, 2):
        halves = []
        for s in (r, r + 1):
            rows = slice(s * DOF, (s + 1) * DOF)
            stack = []
            for d in range(FACES + 1):
                block = field[rows, :] if d == 0 else beside[rows, (d - 1) * E : d * E]
                stack += [masked(block, kinds[2 * d]), masked(block, kinds[2 * d + 1])]
            halves.append(jnp.concatenate(stack, axis=0))
        product = jnp.dot(wide[...], jnp.concatenate(halves, axis=1), preferred_element_type=F32)
        for i in range(2):
            rows = slice((r + i) * DOF, (r + i + 1) * DOF)
            part = rhs[rows, own] - product[:, i * E : (i + 1) * E]
            residual_ref[rows, :] = part
            rounded_ref[rows, :] = part.astype(BF)
    send(picker(pair[...], E), rounded_ref[...], [(message, PAIRS)])


def mate_picker(partner, first, count):
    return jnp.where(iota((count, E), 0) + first == partner, 1.0, 0.0).astype(BF)


def local_kernel(residual_ref, rounded_ref, partner, out_ref, half_ref):
    rest = (residual_ref[...] - rounded_ref[...].astype(F32)).astype(BF)
    local = mate_picker(partner[...], 0, E)
    mates = jnp.dot(rounded_ref[...], local, preferred_element_type=F32)
    mates = mates + jnp.dot(rest, local, preferred_element_type=F32)
    half_ref[...] = residual_ref[...] + mates
    for r in range(RHS):
        out_ref[pl.ds(r, DOF, stride=RHS), :] = residual_ref[r * DOF : (r + 1) * DOF, :]


def coarse_kernel(place_ref, half_ref, incoming, partner, inverse, iterate, solution_ref):
    own = half(place_ref[0])
    mates = lax.dot_general(
        incoming[...], mate_picker(partner[...], E, PAIRS), (((0,), (0,)), ((), ())), preferred_element_type=F32
    )
    coarse = (half_ref[...] + mates).astype(BF)
    for r in range(0, RHS, 2):
        pair = jnp.concatenate([coarse[s * DOF : (s + 1) * DOF, :] for s in (r, r + 1)], axis=1)
        update = jnp.dot(inverse[...], pair, preferred_element_type=F32)
        for i in range(2):
            s = r + i
            solution_ref[pl.ds(s, DOF, stride=RHS), :] = iterate[s * DOF : (s + 1) * DOF, own] + update[:, i * E : (i + 1) * E]


def body(
    rhs,
    guess,
    diag_blocks,
    face_blocks,
    smoother,
    coarse_inverse,
    elem_type,
    face_type,
    neighbours,
    send_near,
    send_far,
    sub_send,
    partner,
    pair_send,
):
    a = lax.axis_index("dom")
    place = jnp.stack([a % 2, (a // 2) % 2]).astype(jnp.int32)
    doms = lax.axis_size("dom")
    rhs = rhs.reshape(ROWS, E)
    guess = guess.reshape(ROWS, E)
    inside = [(i, i + 1) for i in range(0, doms, 2)]
    cross_one = [(i + j, i + j + 2) for i in range(0, doms, 4) for j in range(2)]
    cross_two = [(i + j + 2, i + j + 4) for i in range(0, doms, 4) for j in range(2)]

    def exchange(messages):
        one, two, side = messages
        two = swap(two, "dom", cross_two)
        one = swap(one, "dom", cross_one)
        side = lax.all_to_all(side, "sub", 0, 0, tiled=True)
        return two, one, side

    message_outs = [((n, ROWS), BF) for n in SENT]
    taken = (send_near, send_far, sub_send.reshape(1, -1), elem_type.reshape(1, -1), face_type, neighbours, guess, rhs)
    (mine,) = call(
        first_kernel,
        [((2 * ROWS + INTS, E), BF)],
        *taken,
        remote=len(taken),
        scratch=[pltpu.VMEM(x.shape, x.dtype) for x in taken]
        + [pltpu.VMEM((INTS, E), F32), pltpu.SemaphoreType.DMA((len(taken),))],
        vmem=60,
    )
    other = swap(mine, "dom", inside)
    field, ints, choice, *messages = call(
        pack_kernel,
        [((ROWS, CHIP), BF), ((2, INTS, E), jnp.int32), ((2 * CROSS + SIDE, CHIP), BF)] + message_outs,
        place,
        mine,
        other,
        flops=2 * (2 * CROSS + SIDE) * CHIP * ROWS,
        scalars=1,
    )
    halo = exchange(messages)
    pick, masks, wide, smooth, rhs = call(
        prep_kernel,
        [
            ((KEPT, FACES * CHIP), BF),
            ((2 * FACES + 2, 16, CHIP), BF),
            ((DOF, 2 * DOF * (FACES + 1)), BF),
            ((DOF, 2 * DOF), BF),
            ((ROWS, CHIP), F32),
        ],
        place,
        diag_blocks,
        face_blocks,
        smoother,
        ints,
        other,
        rhs,
        flops=1000000,
        scalars=1,
    )
    work = 2 * ROWS * KEPT * FACES * CHIP + 2 * DOF * 14 * DOF * RHS * CHIP
    before = (guess, other)
    for _ in range(SWEEPS):
        iterate, field, *messages = call(
            sweep_kernel,
            [((ROWS, CHIP), F32), ((ROWS, CHIP), BF)] + message_outs,
            place,
            field,
            *halo,
            pick,
            masks,
            wide,
            smooth,
            rhs,
            choice,
            *before,
            flops=work,
            scalars=1,
        )
        before = (iterate,)
        halo = exchange(messages)
    residual, rounded, message = call(
        residual_kernel,
        [((ROWS, E), F32), ((ROWS, E), BF), ((PAIRS, ROWS), BF)],
        place,
        field,
        *halo,
        pick,
        masks,
        wide,
        rhs,
        pair_send.reshape(1, -1),
        flops=work // 2,
        scalars=1,
    )
    subs = lax.axis_size("sub")
    incoming = swap(message, "sub", [(i, i + 1) for i in range(0, subs, 2)])
    partner = partner.reshape(1, -1)
    residual, coarse = call(
        local_kernel,
        [((ROWS, E), F32), ((ROWS, E), F32)],
        residual,
        rounded,
        partner,
        flops=work // 8,
    )
    (solved,) = call(
        coarse_kernel,
        [((ROWS, E), F32)],
        place,
        coarse,
        incoming,
        partner,
        coarse_inverse,
        iterate,
        flops=work // 8,
        scalars=1,
    )
    shape = (DOF, RHS, E)
    return (solved.reshape(shape), residual.reshape(shape))


SENT = (SIDE + 16, SIDE + 16, SIDE)


def solution(mesh):
    block = P(None, None, ("dom", "sub"))
    flat = P(("dom", "sub"))
    listed = P(None, ("dom", "sub"))
    in_specs = (block, block, P(), P(), P(), P(), flat, listed, listed, listed, listed, flat, flat, flat)
    return jax.shard_map(body, mesh=mesh, in_specs=in_specs, out_specs=(block, block), check_vma=False)
```

```python
import jax
import jax.numpy as jnp
from jax import lax
from jax.experimental import pallas as pl
from jax.experimental.pallas import tpu as pltpu
from jax.sharding import PartitionSpec as P

SWEEPS = 2
DOF = 64
RHS = 8
E = 128
CHIP = 2 * E
FACES = 6
ROWS = DOF * RHS
NEAR = 32
FAR = 8
SUB = 8
PAIRS = 16
CROSS = NEAR + 2 * FAR
SIDE = 4 * 2 * SUB
KEPT = CHIP + 2 * CROSS + SIDE
INTS = 32
BF = jnp.bfloat16
F32 = jnp.float32


def swap(array, axis, pairs):
    count = lax.axis_size(axis)
    route = []
    for low, high in pairs:
        if high < count:
            route += [(low, high), (high, low)]
    return lax.ppermute(array, axis, route)


def spec():
    return pl.BlockSpec(memory_space=pltpu.VMEM)


def call(kernel, outs, *args, flops=0, scalars=0, remote=0, scratch=(), vmem=16):
    specs = [pl.BlockSpec(memory_space=pltpu.SMEM)] * scalars
    specs += [pl.BlockSpec(memory_space=pl.ANY)] * remote
    specs += [spec()] * (len(args) - scalars - remote)
    moved = sum(a.size * a.dtype.itemsize for a in args)
    return pl.pallas_call(
        kernel,
        out_shape=[jax.ShapeDtypeStruct(s, d) for s, d in outs],
        in_specs=specs,
        out_specs=[spec()] * len(outs),
        scratch_shapes=scratch,
        cost_estimate=pl.CostEstimate(flops=flops, bytes_accessed=moved, transcendentals=0),
        compiler_params=pltpu.CompilerParams(vmem_limit_bytes=vmem << 20),
    )(*args)


def iota(shape, dim):
    return lax.broadcasted_iota(jnp.int32, shape, dim)


def half(core):
    return pl.ds(pl.multiple_of(core * E, E), E)


def column(row):
    count = row.shape[1]
    wide = jnp.broadcast_to(row.astype(F32), (count, count))
    kept = jnp.where(iota((count, count), 0) == iota((count, count), 1), wide, 0.0)
    return jnp.sum(kept, axis=1, keepdims=True).astype(jnp.int32)


def picker(row, width):
    count = row.shape[1]
    return jnp.where(iota((count, width), 1) == column(row), 1.0, 0.0).astype(BF)


def send(choice, field, refs):
    rows = lax.dot_general(choice, field, (((1,), (1,)), ((), ())), preferred_element_type=F32).astype(BF)
    start = 0
    for ref, used in refs:
        ref[:used] = rows[start : start + used]
        if ref.shape[0] > used:
            ref[used:] = jnp.zeros((ref.shape[0] - used, ROWS), BF)
        start += used


def first_kernel(*refs):
    sources, message, targets, ints, arrived = refs[:8], refs[8], refs[9:17], refs[17], refs[18]
    copies = [pltpu.make_async_copy(a, b, arrived.at[i]) for i, (a, b) in enumerate(zip(sources, targets))]
    for copy in copies:
        copy.start()
    near, far, sub, elem_type, face_type, neighbours, guess, rhs = targets
    for copy in copies[:6]:
        copy.wait()
    ints[...] = jnp.zeros((INTS, E), F32)
    ints[0:6, :] = neighbours[...].astype(F32)
    ints[8:14, :] = face_type[...].astype(F32)
    ints[14:15, :] = elem_type[...].astype(F32)
    ints[16:18, :NEAR] = near[...].astype(F32)
    ints[18:20, :FAR] = far[...].astype(F32)
    ints[20:21, :SUB] = sub[...].astype(F32)
    message[2 * ROWS :, :] = ints[...].astype(BF)
    for i, field in enumerate((guess, rhs)):
        copies[6 + i].wait()
        blocks = [field[pl.ds(r, DOF, stride=RHS), :].astype(BF) for r in range(RHS)]
        message[i * ROWS : (i + 1) * ROWS, :] = jnp.concatenate(blocks, axis=0)


def pack_kernel(place_ref, mine, other, field_ref, ints_ref, choice_ref, *messages):
    core = place_ref[0]
    odd = place_ref[1] == 1
    field_ref[:, half(core)] = mine[:ROWS, :]
    field_ref[:, half(1 - core)] = other[:ROWS, :]
    ints_ref[core] = mine[2 * ROWS :, :].astype(F32).astype(jnp.int32)
    ints_ref[1 - core] = other[2 * ROWS :, :].astype(F32).astype(jnp.int32)
    low, high = ints_ref[0], ints_ref[1]

    def chosen(near, one, two):
        return picker(near, CHIP), jnp.concatenate([picker(one, CHIP), picker(two + E, CHIP)], axis=0)

    up = (high[17:18, :NEAR] + E, low[19:20, :FAR], high[19:20, :FAR])
    down = (low[16:17, :NEAR], low[18:19, :FAR], high[18:19, :FAR])
    to_one = [jnp.where(odd, d, u) for u, d in zip(up, down)]
    to_two = [jnp.where(odd, u, d) for u, d in zip(up, down)]
    side = jnp.concatenate([picker(low[20:21, :SUB], CHIP), picker(high[20:21, :SUB] + E, CHIP)], axis=0)
    choice = jnp.concatenate([*chosen(*to_one), *chosen(*to_two), side, side, side, side], axis=0)
    choice_ref[...] = choice
    send(choice, field_ref[...], zip(messages, (CROSS, CROSS, SIDE)))


def prep_kernel(place_ref, diag, face, smooth, ints, other, rhs, pick_ref, mask_ref, wide_ref, smooth_ref, rhs_ref):
    core = place_ref[0]
    odd = place_ref[1] == 1
    below = jnp.where(odd, CHIP, CHIP + CROSS)
    above = jnp.where(odd, CHIP + CROSS, CHIP)
    for c in range(2):
        mine, near = ints[c], ints[1 - c]
        listed = near[16:17, :NEAR] if c == 0 else near[17:18, :NEAR]
        inner = jnp.where(iota((E, NEAR), 0) == listed, 1.0, 0.0).astype(BF)
        for d in range(FACES):
            k = mine[d : d + 1, :]
            m = k - 208
            place = CHIP + 2 * CROSS + (m >> 3) * 2 * SUB + c * SUB + (m & 7)
            place = jnp.where(k < 208, above + NEAR + c * FAR + k - 200, place)
            place = jnp.where(k < 200, below + NEAR + c * FAR + k - 192, place)
            place = jnp.where(k < 192, -1 if c == 0 else above + k - 160, place)
            place = jnp.where(k < 160, below + k - 128 if c == 0 else -1, place)
            place = jnp.where(k < E, k + c * E, place)
            lanes = slice(d * CHIP + c * E, d * CHIP + (c + 1) * E)
            hot = jnp.where(iota((KEPT, E), 0) == place, 1.0, 0.0)
            slot = jnp.where(iota((NEAR, E), 0) + (160 if c == 0 else 128) == k, 1.0, 0.0).astype(BF)
            within = jnp.dot(inner, slot, preferred_element_type=F32)
            start = (1 - c) * E
            if start:
                pick_ref[:start, lanes] = hot[:start].astype(BF)
            pick_ref[start : start + E, lanes] = (hot[start : start + E] + within).astype(BF)
            pick_ref[start + E :, lanes] = hot[start + E :].astype(BF)
        for d in range(FACES + 1):
            kinds = mine[14:15, :] if d == 0 else mine[7 + d : 8 + d, :]
            for t in range(2):
                mask = jnp.where(jnp.broadcast_to(kinds, (16, E)) == t, 1.0, 0.0)
                mask_ref[2 * d + t, :, c * E : (c + 1) * E] = mask.astype(BF)
    for d in range(FACES + 1):
        both = (diag[0], diag[1]) if d == 0 else (face[d - 1, 0], face[d - 1, 1])
        wide_ref[:, d * 2 * DOF : (d + 1) * 2 * DOF] = jnp.concatenate(both, axis=1)
    smooth_ref[...] = jnp.concatenate([smooth[0], smooth[1]], axis=1)
    for r in range(RHS):
        rows = slice(r * DOF, (r + 1) * DOF)
        rhs_ref[rows, half(core)] = rhs[pl.ds(r, DOF, stride=RHS), :]
    rhs_ref[:, half(1 - core)] = other[ROWS : 2 * ROWS, :].astype(F32)


def masked(block, mask):
    return block * jnp.concatenate([mask] * (DOF // 16), axis=0)


def extend(field_ref, halo):
    near = jnp.concatenate([ref[:used] for ref, used in zip(halo, (CROSS, CROSS, SIDE))], axis=0)
    return jnp.concatenate([field_ref[...], near.T], axis=1)


def sweep_kernel(place_ref, field_ref, two, one, side, pick, masks, wide, smooth, rhs, choice, *refs):
    core = place_ref[0]
    before, (after, next_field, *messages) = refs[:-5], refs[-5:]
    if len(before) == 2:
        guess, other = before
        for r in range(RHS):
            after[r * DOF : (r + 1) * DOF, half(core)] = guess[pl.ds(r, DOF, stride=RHS), :]
        after[:, half(1 - core)] = other[:ROWS, :].astype(F32)
        before = after
    else:
        (before,) = before
    beside = jnp.dot(extend(field_ref, (one, two, side)), pick[...], preferred_element_type=F32).astype(BF)
    parts = []
    for r in range(RHS):
        rows = slice(r * DOF, (r + 1) * DOF)
        stack = []
        for d in range(FACES + 1):
            block = field_ref[rows, :] if d == 0 else beside[rows, (d - 1) * CHIP : d * CHIP]
            stack += [masked(block, masks[2 * d]), masked(block, masks[2 * d + 1])]
        product = jnp.dot(wide[...], jnp.concatenate(stack, axis=0), preferred_element_type=F32)
        rounded = (rhs[rows, :] - product).astype(BF)
        parts.append(jnp.concatenate([masked(rounded, masks[0]), masked(rounded, masks[1])], axis=0))
    changes = [jnp.dot(smooth[...], part, preferred_element_type=F32) for part in parts]
    new = before[...] + jnp.concatenate(changes, axis=0)
    rounded = new.astype(BF)
    send(choice[...], rounded, zip(messages, (CROSS, CROSS, SIDE)))
    after[...] = new
    next_field[...] = rounded


def residual_kernel(place_ref, field_ref, two, one, side, pick, masks, wide, rhs, pair, residual_ref, rounded_ref, message):
    core = place_ref[0]
    own = half(core)
    extended = extend(field_ref, (one, two, side))
    beside = []
    for d in range(FACES):
        columns = pick[:, pl.ds(pl.multiple_of(d * CHIP + core * E, E), E)]
        beside.append(columns)
    beside = jnp.dot(extended, jnp.concatenate(beside, axis=1), preferred_element_type=F32).astype(BF)
    field = field_ref[:, own]
    kinds = [masks[i, :, own] for i in range(2 * FACES + 2)]
    parts = []
    for r in range(0, RHS, 2):
        halves = []
        for s in (r, r + 1):
            rows = slice(s * DOF, (s + 1) * DOF)
            stack = []
            for d in range(FACES + 1):
                block = field[rows, :] if d == 0 else beside[rows, (d - 1) * E : d * E]
                stack += [masked(block, kinds[2 * d]), masked(block, kinds[2 * d + 1])]
            halves.append(jnp.concatenate(stack, axis=0))
        product = jnp.dot(wide[...], jnp.concatenate(halves, axis=1), preferred_element_type=F32)
        parts += [rhs[(r + i) * DOF : (r + i + 1) * DOF, own] - product[:, i * E : (i + 1) * E] for i in range(2)]
    residual = jnp.concatenate(parts, axis=0)
    rounded = residual.astype(BF)
    send(picker(pair[...], E), rounded, [(message, PAIRS)])
    residual_ref[...] = residual
    rounded_ref[...] = rounded


def mate_picker(partner, first, count):
    return jnp.where(iota((count, E), 0) + first == partner, 1.0, 0.0).astype(BF)


def local_kernel(residual_ref, rounded_ref, partner, out_ref, half_ref):
    residual = residual_ref[...]
    rounded = rounded_ref[...]
    rest = (residual - rounded.astype(F32)).astype(BF)
    local = mate_picker(partner[...], 0, E)
    mates = jnp.dot(rounded, local, preferred_element_type=F32)
    mates = mates + jnp.dot(rest, local, preferred_element_type=F32)
    for r in range(RHS):
        out_ref[pl.ds(r, DOF, stride=RHS), :] = residual[r * DOF : (r + 1) * DOF, :]
    half_ref[...] = residual + mates


def coarse_kernel(place_ref, half_ref, incoming, partner, inverse, iterate, solution_ref):
    own = half(place_ref[0])
    mates = lax.dot_general(
        incoming[...], mate_picker(partner[...], E, PAIRS), (((0,), (0,)), ((), ())), preferred_element_type=F32
    )
    coarse = (half_ref[...] + mates).astype(BF)
    solved = []
    for r in range(0, RHS, 2):
        pair = jnp.concatenate([coarse[s * DOF : (s + 1) * DOF, :] for s in (r, r + 1)], axis=1)
        update = jnp.dot(inverse[...], pair, preferred_element_type=F32)
        solved += [iterate[(r + i) * DOF : (r + i + 1) * DOF, own] + update[:, i * E : (i + 1) * E] for i in range(2)]
    for r in range(RHS):
        solution_ref[pl.ds(r, DOF, stride=RHS), :] = solved[r]


def body(
    rhs,
    guess,
    diag_blocks,
    face_blocks,
    smoother,
    coarse_inverse,
    elem_type,
    face_type,
    neighbours,
    send_near,
    send_far,
    sub_send,
    partner,
    pair_send,
):
    a = lax.axis_index("dom")
    place = jnp.stack([a % 2, (a // 2) % 2]).astype(jnp.int32)
    doms = lax.axis_size("dom")
    rhs = rhs.reshape(ROWS, E)
    guess = guess.reshape(ROWS, E)
    inside = [(i, i + 1) for i in range(0, doms, 2)]
    cross_one = [(i + j, i + j + 2) for i in range(0, doms, 4) for j in range(2)]
    cross_two = [(i + j + 2, i + j + 4) for i in range(0, doms, 4) for j in range(2)]

    def exchange(messages):
        one, two, side = messages
        two = swap(two, "dom", cross_two)
        one = swap(one, "dom", cross_one)
        side = lax.all_to_all(side, "sub", 0, 0, tiled=True)
        return two, one, side

    message_outs = [((n, ROWS), BF) for n in SENT]
    taken = (send_near, send_far, sub_send.reshape(1, -1), elem_type.reshape(1, -1), face_type, neighbours, guess, rhs)
    (mine,) = call(
        first_kernel,
        [((2 * ROWS + INTS, E), BF)],
        *taken,
        remote=len(taken),
        scratch=[pltpu.VMEM(x.shape, x.dtype) for x in taken]
        + [pltpu.VMEM((INTS, E), F32), pltpu.SemaphoreType.DMA((len(taken),))],
        vmem=60,
    )
    other = swap(mine, "dom", inside)
    field, ints, choice, *messages = call(
        pack_kernel,
        [((ROWS, CHIP), BF), ((2, INTS, E), jnp.int32), ((2 * CROSS + SIDE, CHIP), BF)] + message_outs,
        place,
        mine,
        other,
        flops=2 * (2 * CROSS + SIDE) * CHIP * ROWS,
        scalars=1,
    )
    halo = exchange(messages)
    pick, masks, wide, smooth, rhs = call(
        prep_kernel,
        [
            ((KEPT, FACES * CHIP), BF),
            ((2 * FACES + 2, 16, CHIP), BF),
            ((DOF, 2 * DOF * (FACES + 1)), BF),
            ((DOF, 2 * DOF), BF),
            ((ROWS, CHIP), F32),
        ],
        place,
        diag_blocks,
        face_blocks,
        smoother,
        ints,
        other,
        rhs,
        flops=1000000,
        scalars=1,
    )
    work = 2 * ROWS * KEPT * FACES * CHIP + 2 * DOF * 14 * DOF * RHS * CHIP
    before = (guess, other)
    for _ in range(SWEEPS):
        iterate, field, *messages = call(
            sweep_kernel,
            [((ROWS, CHIP), F32), ((ROWS, CHIP), BF)] + message_outs,
            place,
            field,
            *halo,
            pick,
            masks,
            wide,
            smooth,
            rhs,
            choice,
            *before,
            flops=work,
            scalars=1,
        )
        before = (iterate,)
        halo = exchange(messages)
    residual, rounded, message = call(
        residual_kernel,
        [((ROWS, E), F32), ((ROWS, E), BF), ((PAIRS, ROWS), BF)],
        place,
        field,
        *halo,
        pick,
        masks,
        wide,
        rhs,
        pair_send.reshape(1, -1),
        flops=work // 2,
        scalars=1,
    )
    subs = lax.axis_size("sub")
    incoming = swap(message, "sub", [(i, i + 1) for i in range(0, subs, 2)])
    partner = partner.reshape(1, -1)
    residual, coarse = call(
        local_kernel,
        [((ROWS, E), F32), ((ROWS, E), F32)],
        residual,
        rounded,
        partner,
        flops=work // 8,
    )
    (solved,) = call(
        coarse_kernel,
        [((ROWS, E), F32)],
        place,
        coarse,
        incoming,
        partner,
        coarse_inverse,
        iterate,
        flops=work // 8,
        scalars=1,
    )
    shape = (DOF, RHS, E)
    return (solved.reshape(shape), residual.reshape(shape))


SENT = (SIDE + 16, SIDE + 16, SIDE)


def solution(mesh):
    block = P(None, None, ("dom", "sub"))
    flat = P(("dom", "sub"))
    listed = P(None, ("dom", "sub"))
    in_specs = (block, block, P(), P(), P(), P(), flat, listed, listed, listed, listed, flat, flat, flat)
    return jax.shard_map(body, mesh=mesh, in_specs=in_specs, out_specs=(block, block), check_vma=False)
```

```python
import jax
import jax.numpy as jnp
from jax import lax
from jax.experimental import pallas as pl
from jax.experimental.pallas import tpu as pltpu
from jax.sharding import PartitionSpec as P

SWEEPS = 2
DOF = 64
RHS = 8
E = 128
CHIP = 2 * E
FACES = 6
ROWS = DOF * RHS
NEAR = 32
FAR = 8
SUB = 8
PAIRS = 16
CROSS = NEAR + 2 * FAR
SIDE = 4 * 2 * SUB
HALO = 2 * CROSS + SIDE
INTS = 32
BF = jnp.bfloat16
F32 = jnp.float32


def swap(array, axis, pairs):
    count = lax.axis_size(axis)
    route = []
    for low, high in pairs:
        if high < count:
            route += [(low, high), (high, low)]
    return lax.ppermute(array, axis, route)


def spec():
    return pl.BlockSpec(memory_space=pltpu.VMEM)


def call(kernel, outs, *args, flops=0, scalars=0, remote=0, scratch=(), vmem=16):
    specs = [pl.BlockSpec(memory_space=pltpu.SMEM)] * scalars
    specs += [pl.BlockSpec(memory_space=pl.ANY)] * remote
    specs += [spec()] * (len(args) - scalars - remote)
    moved = sum(a.size * a.dtype.itemsize for a in args)
    return pl.pallas_call(
        kernel,
        out_shape=[jax.ShapeDtypeStruct(s, d) for s, d in outs],
        in_specs=specs,
        out_specs=[spec()] * len(outs),
        scratch_shapes=scratch,
        cost_estimate=pl.CostEstimate(flops=flops, bytes_accessed=moved, transcendentals=0),
        compiler_params=pltpu.CompilerParams(vmem_limit_bytes=vmem << 20),
    )(*args)


def iota(shape, dim):
    return lax.broadcasted_iota(jnp.int32, shape, dim)


def column(row):
    count = row.shape[1]
    wide = jnp.broadcast_to(row.astype(F32), (count, count))
    kept = jnp.where(iota((count, count), 0) == iota((count, count), 1), wide, 0.0)
    return jnp.sum(kept, axis=1, keepdims=True).astype(jnp.int32)


def picker(row, width):
    count = row.shape[1]
    return jnp.where(iota((count, width), 1) == column(row), 1.0, 0.0).astype(BF)


def send(choice, field, refs):
    rows = lax.dot_general(choice, field, (((1,), (1,)), ((), ())), preferred_element_type=F32).astype(BF)
    start = 0
    for ref, used in refs:
        ref[:used] = rows[start : start + used]
        if ref.shape[0] > used:
            ref[used:] = jnp.zeros((ref.shape[0] - used, ROWS), BF)
        start += used


def first_kernel(*refs):
    sources, message, targets, ints, arrived = refs[:10], refs[10], refs[11:21], refs[21], refs[22]
    copies = [pltpu.make_async_copy(a, b, arrived.at[i]) for i, (a, b) in enumerate(zip(sources, targets))]
    for copy in copies:
        copy.start()
    near, far, sub, elem_type, face_type, neighbours, pair, partner, guess, rhs = targets
    for copy in copies[:8]:
        copy.wait()
    ints[...] = jnp.zeros((INTS, E), F32)
    ints[0:6, :] = neighbours[...].astype(F32)
    ints[8:14, :] = face_type[...].astype(F32)
    ints[14:15, :] = elem_type[...].astype(F32)
    ints[16:18, :NEAR] = near[...].astype(F32)
    ints[18:20, :FAR] = far[...].astype(F32)
    ints[20:21, :SUB] = sub[...].astype(F32)
    ints[21:22, :PAIRS] = pair[...].astype(F32)
    ints[22:23, :] = partner[...].astype(F32)
    message[2 * ROWS :, :] = ints[...].astype(BF)
    for i, field in enumerate((guess, rhs)):
        copies[8 + i].wait()
        blocks = [field[pl.ds(r, DOF, stride=RHS), :].astype(BF) for r in range(RHS)]
        message[i * ROWS : (i + 1) * ROWS, :] = jnp.concatenate(blocks, axis=0)


def tables(lists, core, odd, local_ref, halo_ref, mask_ref):
    below = jnp.where(odd, 0, CROSS)
    above = jnp.where(odd, CROSS, 0)
    first = core == 0
    slots = []
    for d in range(FACES):
        k = lists[d : d + 1, :]
        m = k - 208
        place = 2 * CROSS + (m >> 3) * 2 * SUB + core * SUB + (m & 7)
        place = jnp.where(k < 208, above + NEAR + core * FAR + k - 200, place)
        place = jnp.where(k < 200, below + NEAR + core * FAR + k - 192, place)
        place = jnp.where(k < 192, jnp.where(first, -1, above + k - 160), place)
        place = jnp.where(k < 160, jnp.where(first, below + k - 128, -1), place)
        place = jnp.where(k < E, -1, place)
        lanes = slice(d * E, (d + 1) * E)
        local_ref[:, lanes] = jnp.where(iota((E, E), 0) == k, 1.0, 0.0).astype(BF)
        halo_ref[:, lanes] = jnp.where(iota((HALO, E), 0) == place, 1.0, 0.0).astype(BF)
        start = jnp.where(first, 160, 128)
        slots.append(jnp.where(iota((NEAR, E), 0) + start == k, 1.0, 0.0).astype(BF))
    for d in range(FACES + 1):
        kinds = lists[14:15, :] if d == 0 else lists[7 + d : 8 + d, :]
        for t in range(2):
            mask_ref[2 * d + t] = jnp.where(jnp.broadcast_to(kinds, (16, E)) == t, 1.0, 0.0).astype(BF)
    return jnp.concatenate(slots, axis=1)


def own_kernel(place_ref, mine, diag, face, smooth, field_ref, ints_ref, slot_ref, local_ref, halo_ref, mask_ref, wide_ref, smooth_ref):
    lists = mine[2 * ROWS :, :].astype(F32).astype(jnp.int32)
    ints_ref[...] = lists
    slot_ref[...] = tables(lists, place_ref[0], place_ref[1] == 1, local_ref, halo_ref, mask_ref)
    field_ref[...] = mine[:ROWS, :]
    for d in range(FACES + 1):
        both = (diag[0], diag[1]) if d == 0 else (face[d - 1, 0], face[d - 1, 1])
        wide_ref[:, d * 2 * DOF : (d + 1) * 2 * DOF] = jnp.concatenate(both, axis=1)
    smooth_ref[...] = jnp.concatenate([smooth[0], smooth[1]], axis=1)


def pack_kernel(place_ref, own_field, own_lists, own_slots, other, field_ref, choice_ref, inner_ref, outer_ref, local_ref, halo_ref, mask_ref, *messages):
    core = place_ref[0]
    first = core == 0
    odd = place_ref[1] == 1
    mine = own_lists[...]
    theirs = other[2 * ROWS :, :].astype(F32).astype(jnp.int32)
    low = jnp.where(first, mine, theirs)
    high = jnp.where(first, theirs, mine)
    low_at, high_at = core * E, (1 - core) * E
    field = jnp.concatenate([own_field[...], other[:ROWS, :]], axis=1)

    def chosen(near, one, two):
        return picker(near, CHIP), jnp.concatenate([picker(one + low_at, CHIP), picker(two + high_at, CHIP)], axis=0)

    up = (high[17:18, :NEAR] + high_at, low[19:20, :FAR], high[19:20, :FAR])
    down = (low[16:17, :NEAR] + low_at, low[18:19, :FAR], high[18:19, :FAR])
    to_one = [jnp.where(odd, d, u) for u, d in zip(up, down)]
    to_two = [jnp.where(odd, u, d) for u, d in zip(up, down)]
    side = jnp.concatenate([picker(low[20:21, :SUB] + low_at, CHIP), picker(high[20:21, :SUB] + high_at, CHIP)], axis=0)
    choice = jnp.concatenate([*chosen(*to_one), *chosen(*to_two), side, side, side, side], axis=0)
    send(choice, field, zip(messages, (CROSS, CROSS, SIDE)))
    choice_ref[...] = choice
    field_ref[...] = field
    their_slots = tables(theirs, 1 - core, odd, local_ref, halo_ref, mask_ref)
    listed = jnp.where(first, theirs[16:17, :NEAR], theirs[17:18, :NEAR])
    inner = jnp.where(iota((E, NEAR), 0) == listed, 1.0, 0.0).astype(BF)
    inner_ref[...] = jnp.dot(inner, own_slots[...], preferred_element_type=F32).astype(BF)
    listed = jnp.where(first, mine[17:18, :NEAR], mine[16:17, :NEAR])
    outer = jnp.where(iota((E, NEAR), 0) == listed, 1.0, 0.0).astype(BF)
    outer_ref[...] = jnp.dot(outer, their_slots, preferred_element_type=F32).astype(BF)


def masked(block, mask):
    return block * jnp.concatenate([mask] * (DOF // 16), axis=0)


def extend(field_ref, halo):
    near = jnp.concatenate([ref[:used] for ref, used in zip(halo, (CROSS, CROSS, SIDE))], axis=0)
    return jnp.concatenate([field_ref[...], near.T], axis=1)


def select(extended, *blocks):
    columns = jnp.concatenate([block[...] for block in blocks], axis=0)
    return jnp.dot(extended, columns, preferred_element_type=F32).astype(BF)


def sweep_kernel(field_ref, two, one, side, *refs):
    own_local, own_halo, own_masks, inner, outer, local, halo, masks, wide, smooth, rhs, other, choice, *refs = refs
    before, (after, next_field, *messages) = refs[:-5], refs[-5:]
    extended = extend(field_ref, (one, two, side))
    mine = select(extended, own_local, inner, own_halo)
    theirs = select(extended, outer, local, halo)
    kinds = [jnp.concatenate([own_masks[i], masks[i]], axis=1) for i in range(2 * FACES + 2)]
    parts = []
    for r in range(RHS):
        rows = slice(r * DOF, (r + 1) * DOF)
        stack = []
        for d in range(FACES + 1):
            lanes = slice((d - 1) * E, d * E)
            block = field_ref[rows, :] if d == 0 else jnp.concatenate([mine[rows, lanes], theirs[rows, lanes]], axis=1)
            stack += [masked(block, kinds[2 * d]), masked(block, kinds[2 * d + 1])]
        product = jnp.dot(wide[...], jnp.concatenate(stack, axis=0), preferred_element_type=F32)
        given = other[ROWS + r * DOF : ROWS + (r + 1) * DOF, :].astype(F32)
        given = jnp.concatenate([rhs[pl.ds(r, DOF, stride=RHS), :], given], axis=1)
        rounded = (given - product).astype(BF)
        parts.append(jnp.concatenate([masked(rounded, kinds[0]), masked(rounded, kinds[1])], axis=0))
    changes = jnp.concatenate([jnp.dot(smooth[...], part, preferred_element_type=F32) for part in parts], axis=0)
    if len(before) == 1 and before[0].shape[1] == CHIP:
        old = before[0][...]
    else:
        own = jnp.concatenate([before[0][pl.ds(r, DOF, stride=RHS), :] for r in range(RHS)], axis=0)
        old = jnp.concatenate([own, other[:ROWS, :].astype(F32)], axis=1)
    new = old + changes
    rounded = new.astype(BF)
    send(choice[...], rounded, zip(messages, (CROSS, CROSS, SIDE)))
    after[...] = new
    next_field[...] = rounded


def residual_kernel(field_ref, two, one, side, own_local, inner, own_halo, masks, wide, rhs, lists, residual_ref, rounded_ref, message):
    beside = select(extend(field_ref, (one, two, side)), own_local, inner, own_halo)
    parts = []
    for r in range(0, RHS, 2):
        halves = []
        for s in (r, r + 1):
            rows = slice(s * DOF, (s + 1) * DOF)
            stack = []
            for d in range(FACES + 1):
                block = field_ref[rows, :E] if d == 0 else beside[rows, (d - 1) * E : d * E]
                stack += [masked(block, masks[2 * d]), masked(block, masks[2 * d + 1])]
            halves.append(jnp.concatenate(stack, axis=0))
        product = jnp.dot(wide[...], jnp.concatenate(halves, axis=1), preferred_element_type=F32)
        parts += [rhs[pl.ds(r + i, DOF, stride=RHS), :] - product[:, i * E : (i + 1) * E] for i in range(2)]
    residual = jnp.concatenate(parts, axis=0)
    rounded = residual.astype(BF)
    send(picker(lists[21:22, :PAIRS], E), rounded, [(message, PAIRS)])
    residual_ref[...] = residual
    rounded_ref[...] = rounded


def mate_picker(partner, first, count):
    return jnp.where(iota((count, E), 0) + first == partner, 1.0, 0.0).astype(BF)


def local_kernel(residual_ref, rounded_ref, lists, out_ref, half_ref):
    residual = residual_ref[...]
    rounded = rounded_ref[...]
    rest = (residual - rounded.astype(F32)).astype(BF)
    local = mate_picker(lists[22:23, :], 0, E)
    mates = jnp.dot(rounded, local, preferred_element_type=F32)
    mates = mates + jnp.dot(rest, local, preferred_element_type=F32)
    for r in range(RHS):
        out_ref[pl.ds(r, DOF, stride=RHS), :] = residual[r * DOF : (r + 1) * DOF, :]
    half_ref[...] = residual + mates


def coarse_kernel(half_ref, incoming, lists, inverse, iterate, solution_ref):
    mates = lax.dot_general(
        incoming[...], mate_picker(lists[22:23, :], E, PAIRS), (((0,), (0,)), ((), ())), preferred_element_type=F32
    )
    coarse = (half_ref[...] + mates).astype(BF)
    solved = []
    for r in range(0, RHS, 2):
        pair = jnp.concatenate([coarse[s * DOF : (s + 1) * DOF, :] for s in (r, r + 1)], axis=1)
        update = jnp.dot(inverse[...], pair, preferred_element_type=F32)
        solved += [iterate[(r + i) * DOF : (r + i + 1) * DOF, :E] + update[:, i * E : (i + 1) * E] for i in range(2)]
    for r in range(RHS):
        solution_ref[pl.ds(r, DOF, stride=RHS), :] = solved[r]


def body(
    rhs,
    guess,
    diag_blocks,
    face_blocks,
    smoother,
    coarse_inverse,
    elem_type,
    face_type,
    neighbours,
    send_near,
    send_far,
    sub_send,
    partner,
    pair_send,
):
    a = lax.axis_index("dom")
    place = jnp.stack([a % 2, (a // 2) % 2]).astype(jnp.int32)
    doms = lax.axis_size("dom")
    rhs = rhs.reshape(ROWS, E)
    guess = guess.reshape(ROWS, E)
    inside = [(i, i + 1) for i in range(0, doms, 2)]
    cross_one = [(i + j, i + j + 2) for i in range(0, doms, 4) for j in range(2)]
    cross_two = [(i + j + 2, i + j + 4) for i in range(0, doms, 4) for j in range(2)]

    def exchange(messages):
        one, two, side = messages
        two = swap(two, "dom", cross_two)
        one = swap(one, "dom", cross_one)
        side = lax.all_to_all(side, "sub", 0, 0, tiled=True)
        return two, one, side

    message_outs = [((n, ROWS), BF) for n in SENT]
    taken = (send_near, send_far, sub_send.reshape(1, -1), elem_type.reshape(1, -1), face_type, neighbours)
    taken += (pair_send.reshape(1, -1), partner.reshape(1, -1), guess, rhs)
    (mine,) = call(
        first_kernel,
        [((2 * ROWS + INTS, E), BF)],
        *taken,
        remote=len(taken),
        scratch=[pltpu.VMEM(x.shape, x.dtype) for x in taken]
        + [pltpu.VMEM((INTS, E), F32), pltpu.SemaphoreType.DMA((len(taken),))],
        vmem=60,
    )
    other = swap(mine, "dom", inside)
    table_outs = [((E, FACES * E), BF), ((HALO, FACES * E), BF), ((2 * FACES + 2, 16, E), BF)]
    own_field, own_lists, own_slots, own_local, own_halo, own_masks, wide, smooth = call(
        own_kernel,
        [((ROWS, E), BF), ((INTS, E), jnp.int32), ((NEAR, FACES * E), BF)]
        + table_outs
        + [((DOF, 2 * DOF * (FACES + 1)), BF), ((DOF, 2 * DOF), BF)],
        place,
        mine,
        diag_blocks,
        face_blocks,
        smoother,
        flops=1000000,
        scalars=1,
    )
    field, choice, inner, outer, local, halo, masks, *messages = call(
        pack_kernel,
        [((ROWS, CHIP), BF), ((HALO, CHIP), BF), ((E, FACES * E), BF), ((E, FACES * E), BF)] + table_outs + message_outs,
        place,
        own_field,
        own_lists,
        own_slots,
        other,
        flops=2 * HALO * CHIP * ROWS,
        scalars=1,
    )
    brought = exchange(messages)
    work = 2 * ROWS * (CHIP + HALO) * FACES * CHIP + 2 * DOF * 14 * DOF * RHS * CHIP
    iterate = guess
    for _ in range(SWEEPS):
        iterate, field, *messages = call(
            sweep_kernel,
            [((ROWS, CHIP), F32), ((ROWS, CHIP), BF)] + message_outs,
            field,
            *brought,
            own_local,
            own_halo,
            own_masks,
            inner,
            outer,
            local,
            halo,
            masks,
            wide,
            smooth,
            rhs,
            other,
            choice,
            iterate,
            flops=work,
        )
        brought = exchange(messages)
    residual, rounded, message = call(
        residual_kernel,
        [((ROWS, E), F32), ((ROWS, E), BF), ((PAIRS, ROWS), BF)],
        field,
        *brought,
        own_local,
        inner,
        own_halo,
        own_masks,
        wide,
        rhs,
        own_lists,
        flops=work // 2,
    )
    subs = lax.axis_size("sub")
    incoming = swap(message, "sub", [(i, i + 1) for i in range(0, subs, 2)])
    residual, coarse = call(
        local_kernel,
        [((ROWS, E), F32), ((ROWS, E), F32)],
        residual,
        rounded,
        own_lists,
        flops=work // 8,
    )
    (solved,) = call(
        coarse_kernel,
        [((ROWS, E), F32)],
        coarse,
        incoming,
        own_lists,
        coarse_inverse,
        iterate,
        flops=work // 8,
    )
    shape = (DOF, RHS, E)
    return (solved.reshape(shape), residual.reshape(shape))


SENT = (SIDE + 16, SIDE + 16, SIDE)


def solution(mesh):
    block = P(None, None, ("dom", "sub"))
    flat = P(("dom", "sub"))
    listed = P(None, ("dom", "sub"))
    in_specs = (block, block, P(), P(), P(), P(), flat, listed, listed, listed, listed, flat, flat, flat)
    return jax.shard_map(body, mesh=mesh, in_specs=in_specs, out_specs=(block, block), check_vma=False)
```

```python
import jax
import jax.numpy as jnp
from jax import lax
from jax.experimental import pallas as pl
from jax.experimental.pallas import tpu as pltpu
from jax.sharding import PartitionSpec as P

SWEEPS = 2
DOF = 64
RHS = 8
E = 128
CHIP = 2 * E
FACES = 6
ROWS = DOF * RHS
NEAR = 32
FAR = 8
SUB = 8
PAIRS = 16
CROSS = NEAR + 2 * FAR
SIDE = 4 * 2 * SUB
HALO = 2 * CROSS + SIDE
WIDE = 2 * DOF * (FACES + 1)
INTS = 32
BF = jnp.bfloat16
F32 = jnp.float32


def swap(array, axis, pairs):
    count = lax.axis_size(axis)
    route = []
    for low, high in pairs:
        if high < count:
            route += [(low, high), (high, low)]
    return lax.ppermute(array, axis, route)


def spec():
    return pl.BlockSpec(memory_space=pltpu.VMEM)


def call(kernel, outs, *args, flops=0, scalars=0, remote=0, scratch=(), vmem=16):
    specs = [pl.BlockSpec(memory_space=pltpu.SMEM)] * scalars
    specs += [pl.BlockSpec(memory_space=pl.ANY)] * remote
    specs += [spec()] * (len(args) - scalars - remote)
    moved = sum(a.size * a.dtype.itemsize for a in args)
    return pl.pallas_call(
        kernel,
        out_shape=[jax.ShapeDtypeStruct(s, d) for s, d in outs],
        in_specs=specs,
        out_specs=[spec()] * len(outs),
        scratch_shapes=scratch,
        cost_estimate=pl.CostEstimate(flops=flops, bytes_accessed=moved, transcendentals=0),
        compiler_params=pltpu.CompilerParams(vmem_limit_bytes=vmem << 20),
    )(*args)


def iota(shape, dim):
    return lax.broadcasted_iota(jnp.int32, shape, dim)


def column(row):
    count = row.shape[1]
    wide = jnp.broadcast_to(row.astype(F32), (count, count))
    kept = jnp.where(iota((count, count), 0) == iota((count, count), 1), wide, 0.0)
    return jnp.sum(kept, axis=1, keepdims=True).astype(jnp.int32)


def picker(row, width):
    count = row.shape[1]
    return jnp.where(iota((count, width), 1) == column(row), 1.0, 0.0).astype(BF)


def send(choice, field, refs):
    rows = lax.dot_general(choice, field, (((1,), (1,)), ((), ())), preferred_element_type=F32).astype(BF)
    start = 0
    for ref, used in refs:
        ref[:used] = rows[start : start + used]
        if ref.shape[0] > used:
            ref[used:] = jnp.zeros((ref.shape[0] - used, ROWS), BF)
        start += used


def first_kernel(*refs):
    sources, (message, wide_ref), targets, (ints, arrived) = refs[:13], refs[13:15], refs[15:28], refs[28:]
    copies = [pltpu.make_async_copy(a, b, arrived.at[i]) for i, (a, b) in enumerate(zip(sources, targets))]
    for copy in copies:
        copy.start()
    near, far, sub, elem_type, face_type, neighbours, pair, partner, guess, rhs, diag, face, smooth = targets
    for copy in copies[:8]:
        copy.wait()
    ints[...] = jnp.zeros((INTS, E), F32)
    ints[0:6, :] = neighbours[...].astype(F32)
    ints[8:14, :] = face_type[...].astype(F32)
    ints[14:15, :] = elem_type[...].astype(F32)
    ints[16:18, :NEAR] = near[...].astype(F32)
    ints[18:20, :FAR] = far[...].astype(F32)
    ints[20:21, :SUB] = sub[...].astype(F32)
    ints[21:22, :PAIRS] = pair[...].astype(F32)
    ints[22:23, :] = partner[...].astype(F32)
    message[2 * ROWS :, :] = ints[...].astype(BF)
    for i, field in enumerate((guess, rhs)):
        copies[8 + i].wait()
        blocks = [field[pl.ds(r, DOF, stride=RHS), :].astype(BF) for r in range(RHS)]
        message[i * ROWS : (i + 1) * ROWS, :] = jnp.concatenate(blocks, axis=0)
    for copy in copies[10:]:
        copy.wait()
    for d in range(FACES + 1):
        both = (diag[0], diag[1]) if d == 0 else (face[d - 1, 0], face[d - 1, 1])
        wide_ref[:, d * 2 * DOF : (d + 1) * 2 * DOF] = jnp.concatenate(both, axis=1)
    wide_ref[:, WIDE:] = jnp.concatenate([smooth[0], smooth[1]], axis=1)


def tables(lists, core, odd, local_ref, halo_ref, mask_ref):
    below = jnp.where(odd, 0, CROSS)
    above = jnp.where(odd, CROSS, 0)
    first = core == 0
    slots = []
    for d in range(FACES):
        k = lists[d : d + 1, :]
        m = k - 208
        place = 2 * CROSS + (m >> 3) * 2 * SUB + core * SUB + (m & 7)
        place = jnp.where(k < 208, above + NEAR + core * FAR + k - 200, place)
        place = jnp.where(k < 200, below + NEAR + core * FAR + k - 192, place)
        place = jnp.where(k < 192, jnp.where(first, -1, above + k - 160), place)
        place = jnp.where(k < 160, jnp.where(first, below + k - 128, -1), place)
        place = jnp.where(k < E, -1, place)
        lanes = slice(d * E, (d + 1) * E)
        local_ref[:, lanes] = jnp.where(iota((E, E), 0) == k, 1.0, 0.0).astype(BF)
        halo_ref[:, lanes] = jnp.where(iota((HALO, E), 0) == place, 1.0, 0.0).astype(BF)
        start = jnp.where(first, 160, 128)
        slots.append(jnp.where(iota((NEAR, E), 0) + start == k, 1.0, 0.0).astype(BF))
    for d in range(FACES + 1):
        kinds = lists[14:15, :] if d == 0 else lists[7 + d : 8 + d, :]
        for t in range(2):
            mask_ref[2 * d + t] = jnp.where(jnp.broadcast_to(kinds, (16, E)) == t, 1.0, 0.0).astype(BF)
    return jnp.concatenate(slots, axis=1)


def own_kernel(place_ref, mine, field_ref, ints_ref, slot_ref, local_ref, halo_ref, mask_ref):
    lists = mine[2 * ROWS :, :].astype(F32).astype(jnp.int32)
    ints_ref[...] = lists
    slot_ref[...] = tables(lists, place_ref[0], place_ref[1] == 1, local_ref, halo_ref, mask_ref)
    field_ref[...] = mine[:ROWS, :]


def pack_kernel(place_ref, own_field, own_lists, own_slots, other, field_ref, choice_ref, inner_ref, outer_ref, local_ref, halo_ref, mask_ref, *messages):
    core = place_ref[0]
    first = core == 0
    odd = place_ref[1] == 1
    mine = own_lists[...]
    theirs = other[2 * ROWS :, :].astype(F32).astype(jnp.int32)
    low = jnp.where(first, mine, theirs)
    high = jnp.where(first, theirs, mine)
    low_at, high_at = core * E, (1 - core) * E
    field = jnp.concatenate([own_field[...], other[:ROWS, :]], axis=1)

    def chosen(near, one, two):
        return picker(near, CHIP), jnp.concatenate([picker(one + low_at, CHIP), picker(two + high_at, CHIP)], axis=0)

    up = (high[17:18, :NEAR] + high_at, low[19:20, :FAR], high[19:20, :FAR])
    down = (low[16:17, :NEAR] + low_at, low[18:19, :FAR], high[18:19, :FAR])
    to_one = [jnp.where(odd, d, u) for u, d in zip(up, down)]
    to_two = [jnp.where(odd, u, d) for u, d in zip(up, down)]
    side = jnp.concatenate([picker(low[20:21, :SUB] + low_at, CHIP), picker(high[20:21, :SUB] + high_at, CHIP)], axis=0)
    choice = jnp.concatenate([*chosen(*to_one), *chosen(*to_two), side, side, side, side], axis=0)
    send(choice, field, zip(messages, (CROSS, CROSS, SIDE)))
    choice_ref[...] = choice
    field_ref[...] = field
    their_slots = tables(theirs, 1 - core, odd, local_ref, halo_ref, mask_ref)
    listed = jnp.where(first, theirs[16:17, :NEAR], theirs[17:18, :NEAR])
    inner = jnp.where(iota((E, NEAR), 0) == listed, 1.0, 0.0).astype(BF)
    inner_ref[...] = jnp.dot(inner, own_slots[...], preferred_element_type=F32).astype(BF)
    listed = jnp.where(first, mine[17:18, :NEAR], mine[16:17, :NEAR])
    outer = jnp.where(iota((E, NEAR), 0) == listed, 1.0, 0.0).astype(BF)
    outer_ref[...] = jnp.dot(outer, their_slots, preferred_element_type=F32).astype(BF)


def masked(block, mask):
    return block * jnp.concatenate([mask] * (DOF // 16), axis=0)


def extend(field_ref, halo):
    near = jnp.concatenate([ref[:used] for ref, used in zip(halo, (CROSS, CROSS, SIDE))], axis=0)
    return jnp.concatenate([field_ref[...], near.T], axis=1)


def select(extended, *blocks):
    columns = jnp.concatenate([block[...] for block in blocks], axis=0)
    return jnp.dot(extended, columns, preferred_element_type=F32).astype(BF)


def sweep_kernel(field_ref, two, one, side, *refs):
    own_local, own_halo, own_masks, inner, outer, local, halo, masks, wide, rhs, other, choice, *refs = refs
    before, (after, next_field, *messages) = refs[:-5], refs[-5:]
    extended = extend(field_ref, (one, two, side))
    mine = select(extended, own_local, inner, own_halo)
    theirs = select(extended, outer, local, halo)
    kinds = [jnp.concatenate([own_masks[i], masks[i]], axis=1) for i in range(2 * FACES + 2)]
    parts = []
    for r in range(RHS):
        rows = slice(r * DOF, (r + 1) * DOF)
        stack = []
        for d in range(FACES + 1):
            lanes = slice((d - 1) * E, d * E)
            block = field_ref[rows, :] if d == 0 else jnp.concatenate([mine[rows, lanes], theirs[rows, lanes]], axis=1)
            stack += [masked(block, kinds[2 * d]), masked(block, kinds[2 * d + 1])]
        product = jnp.dot(wide[:, :WIDE], jnp.concatenate(stack, axis=0), preferred_element_type=F32)
        given = other[ROWS + r * DOF : ROWS + (r + 1) * DOF, :].astype(F32)
        given = jnp.concatenate([rhs[pl.ds(r, DOF, stride=RHS), :], given], axis=1)
        rounded = (given - product).astype(BF)
        parts.append(jnp.concatenate([masked(rounded, kinds[0]), masked(rounded, kinds[1])], axis=0))
    changes = jnp.concatenate([jnp.dot(wide[:, WIDE:], part, preferred_element_type=F32) for part in parts], axis=0)
    if len(before) == 1 and before[0].shape[1] == CHIP:
        old = before[0][...]
    else:
        own = jnp.concatenate([before[0][pl.ds(r, DOF, stride=RHS), :] for r in range(RHS)], axis=0)
        old = jnp.concatenate([own, other[:ROWS, :].astype(F32)], axis=1)
    new = old + changes
    rounded = new.astype(BF)
    send(choice[...], rounded, zip(messages, (CROSS, CROSS, SIDE)))
    after[...] = new
    next_field[...] = rounded


def residual_kernel(field_ref, two, one, side, own_local, inner, own_halo, masks, wide, rhs, lists, residual_ref, rounded_ref, message):
    beside = select(extend(field_ref, (one, two, side)), own_local, inner, own_halo)
    parts = []
    for r in range(0, RHS, 2):
        halves = []
        for s in (r, r + 1):
            rows = slice(s * DOF, (s + 1) * DOF)
            stack = []
            for d in range(FACES + 1):
                block = field_ref[rows, :E] if d == 0 else beside[rows, (d - 1) * E : d * E]
                stack += [masked(block, masks[2 * d]), masked(block, masks[2 * d + 1])]
            halves.append(jnp.concatenate(stack, axis=0))
        product = jnp.dot(wide[:, :WIDE], jnp.concatenate(halves, axis=1), preferred_element_type=F32)
        parts += [rhs[pl.ds(r + i, DOF, stride=RHS), :] - product[:, i * E : (i + 1) * E] for i in range(2)]
    residual = jnp.concatenate(parts, axis=0)
    rounded = residual.astype(BF)
    send(picker(lists[21:22, :PAIRS], E), rounded, [(message, PAIRS)])
    residual_ref[...] = residual
    rounded_ref[...] = rounded


def mate_picker(partner, first, count):
    return jnp.where(iota((count, E), 0) + first == partner, 1.0, 0.0).astype(BF)


def local_kernel(residual_ref, rounded_ref, lists, out_ref, half_ref):
    residual = residual_ref[...]
    rounded = rounded_ref[...]
    rest = (residual - rounded.astype(F32)).astype(BF)
    local = mate_picker(lists[22:23, :], 0, E)
    mates = jnp.dot(rounded, local, preferred_element_type=F32)
    mates = mates + jnp.dot(rest, local, preferred_element_type=F32)
    for r in range(RHS):
        out_ref[pl.ds(r, DOF, stride=RHS), :] = residual[r * DOF : (r + 1) * DOF, :]
    half_ref[...] = residual + mates


def coarse_kernel(half_ref, incoming, lists, inverse, iterate, solution_ref):
    mates = lax.dot_general(
        incoming[...], mate_picker(lists[22:23, :], E, PAIRS), (((0,), (0,)), ((), ())), preferred_element_type=F32
    )
    coarse = (half_ref[...] + mates).astype(BF)
    solved = []
    for r in range(0, RHS, 2):
        pair = jnp.concatenate([coarse[s * DOF : (s + 1) * DOF, :] for s in (r, r + 1)], axis=1)
        update = jnp.dot(inverse[...], pair, preferred_element_type=F32)
        solved += [iterate[(r + i) * DOF : (r + i + 1) * DOF, :E] + update[:, i * E : (i + 1) * E] for i in range(2)]
    for r in range(RHS):
        solution_ref[pl.ds(r, DOF, stride=RHS), :] = solved[r]


def body(
    rhs,
    guess,
    diag_blocks,
    face_blocks,
    smoother,
    coarse_inverse,
    elem_type,
    face_type,
    neighbours,
    send_near,
    send_far,
    sub_send,
    partner,
    pair_send,
):
    a = lax.axis_index("dom")
    place = jnp.stack([a % 2, (a // 2) % 2]).astype(jnp.int32)
    doms = lax.axis_size("dom")
    rhs = rhs.reshape(ROWS, E)
    guess = guess.reshape(ROWS, E)
    inside = [(i, i + 1) for i in range(0, doms, 2)]
    cross_one = [(i + j, i + j + 2) for i in range(0, doms, 4) for j in range(2)]
    cross_two = [(i + j + 2, i + j + 4) for i in range(0, doms, 4) for j in range(2)]

    def exchange(messages):
        one, two, side = messages
        two = swap(two, "dom", cross_two)
        one = swap(one, "dom", cross_one)
        side = lax.all_to_all(side, "sub", 0, 0, tiled=True)
        return two, one, side

    message_outs = [((n, ROWS), BF) for n in SENT]
    taken = (send_near, send_far, sub_send.reshape(1, -1), elem_type.reshape(1, -1), face_type, neighbours)
    taken += (pair_send.reshape(1, -1), partner.reshape(1, -1), guess, rhs)
    taken += (diag_blocks, face_blocks, smoother)
    mine, wide = call(
        first_kernel,
        [((2 * ROWS + INTS, E), BF), ((DOF, WIDE + 2 * DOF), BF)],
        *taken,
        remote=len(taken),
        scratch=[pltpu.VMEM(x.shape, x.dtype) for x in taken]
        + [pltpu.VMEM((INTS, E), F32), pltpu.SemaphoreType.DMA((len(taken),))],
        vmem=60,
    )
    other = swap(mine, "dom", inside)
    table_outs = [((E, FACES * E), BF), ((HALO, FACES * E), BF), ((2 * FACES + 2, 16, E), BF)]
    own_field, own_lists, own_slots, own_local, own_halo, own_masks = call(
        own_kernel,
        [((ROWS, E), BF), ((INTS, E), jnp.int32), ((NEAR, FACES * E), BF)] + table_outs,
        place,
        mine,
        flops=1000000,
        scalars=1,
    )
    field, choice, inner, outer, local, halo, masks, *messages = call(
        pack_kernel,
        [((ROWS, CHIP), BF), ((HALO, CHIP), BF), ((E, FACES * E), BF), ((E, FACES * E), BF)] + table_outs + message_outs,
        place,
        own_field,
        own_lists,
        own_slots,
        other,
        flops=2 * HALO * CHIP * ROWS,
        scalars=1,
    )
    brought = exchange(messages)
    work = 2 * ROWS * (CHIP + HALO) * FACES * CHIP + 2 * DOF * 14 * DOF * RHS * CHIP
    iterate = guess
    for _ in range(SWEEPS):
        iterate, field, *messages = call(
            sweep_kernel,
            [((ROWS, CHIP), F32), ((ROWS, CHIP), BF)] + message_outs,
            field,
            *brought,
            own_local,
            own_halo,
            own_masks,
            inner,
            outer,
            local,
            halo,
            masks,
            wide,
            rhs,
            other,
            choice,
            iterate,
            flops=work,
        )
        brought = exchange(messages)
    residual, rounded, message = call(
        residual_kernel,
        [((ROWS, E), F32), ((ROWS, E), BF), ((PAIRS, ROWS), BF)],
        field,
        *brought,
        own_local,
        inner,
        own_halo,
        own_masks,
        wide,
        rhs,
        own_lists,
        flops=work // 2,
    )
    subs = lax.axis_size("sub")
    incoming = swap(message, "sub", [(i, i + 1) for i in range(0, subs, 2)])
    residual, coarse = call(
        local_kernel,
        [((ROWS, E), F32), ((ROWS, E), F32)],
        residual,
        rounded,
        own_lists,
        flops=work // 8,
    )
    (solved,) = call(
        coarse_kernel,
        [((ROWS, E), F32)],
        coarse,
        incoming,
        own_lists,
        coarse_inverse,
        iterate,
        flops=work // 8,
    )
    shape = (DOF, RHS, E)
    return (solved.reshape(shape), residual.reshape(shape))


SENT = (SIDE + 16, SIDE + 16, SIDE)


def solution(mesh):
    block = P(None, None, ("dom", "sub"))
    flat = P(("dom", "sub"))
    listed = P(None, ("dom", "sub"))
    in_specs = (block, block, P(), P(), P(), P(), flat, listed, listed, listed, listed, flat, flat, flat)
    return jax.shard_map(body, mesh=mesh, in_specs=in_specs, out_specs=(block, block), check_vma=False)
```

```python
import jax
import jax.numpy as jnp
from jax import lax
from jax.experimental import pallas as pl
from jax.experimental.pallas import tpu as pltpu
from jax.sharding import PartitionSpec as P

SWEEPS = 2
DOF = 64
RHS = 8
E = 128
CHIP = 2 * E
FACES = 6
ROWS = DOF * RHS
NEAR = 32
FAR = 8
SUB = 8
PAIRS = 16
CROSS = NEAR + 2 * FAR
SIDE = 4 * 2 * SUB
HALO = 2 * CROSS + SIDE
WIDE = 2 * DOF * (FACES + 1)
INTS = 32
BF = jnp.bfloat16
F32 = jnp.float32


def swap(array, axis, pairs):
    count = lax.axis_size(axis)
    route = []
    for low, high in pairs:
        if high < count:
            route += [(low, high), (high, low)]
    return lax.ppermute(array, axis, route)


def spec():
    return pl.BlockSpec(memory_space=pltpu.VMEM)


def call(kernel, outs, *args, flops=0, scalars=0, remote=0, scratch=(), vmem=16):
    specs = [pl.BlockSpec(memory_space=pltpu.SMEM)] * scalars
    specs += [pl.BlockSpec(memory_space=pl.ANY)] * remote
    specs += [spec()] * (len(args) - scalars - remote)
    moved = sum(a.size * a.dtype.itemsize for a in args)
    return pl.pallas_call(
        kernel,
        out_shape=[jax.ShapeDtypeStruct(s, d) for s, d in outs],
        in_specs=specs,
        out_specs=[spec()] * len(outs),
        scratch_shapes=scratch,
        cost_estimate=pl.CostEstimate(flops=flops, bytes_accessed=moved, transcendentals=0),
        compiler_params=pltpu.CompilerParams(vmem_limit_bytes=vmem << 20),
    )(*args)


def iota(shape, dim):
    return lax.broadcasted_iota(jnp.int32, shape, dim)


def column(row):
    count = row.shape[1]
    wide = jnp.broadcast_to(row.astype(F32), (count, count))
    kept = jnp.where(iota((count, count), 0) == iota((count, count), 1), wide, 0.0)
    return jnp.sum(kept, axis=1, keepdims=True).astype(jnp.int32)


def picker(row, width):
    count = row.shape[1]
    return jnp.where(iota((count, width), 1) == column(row), 1.0, 0.0).astype(BF)


def send(choice, field, refs):
    rows = lax.dot_general(choice, field, (((1,), (1,)), ((), ())), preferred_element_type=F32).astype(BF)
    start = 0
    for ref, used in refs:
        ref[:used] = rows[start : start + used]
        if ref.shape[0] > used:
            ref[used:] = jnp.zeros((ref.shape[0] - used, ROWS), BF)
        start += used


def first_kernel(*refs):
    sources, (message, wide_ref), targets, (ints, arrived) = refs[:13], refs[13:15], refs[15:28], refs[28:]
    copies = [pltpu.make_async_copy(a, b, arrived.at[i]) for i, (a, b) in enumerate(zip(sources, targets))]
    for copy in copies:
        copy.start()
    near, far, sub, elem_type, face_type, neighbours, pair, partner, guess, rhs, diag, face, smooth = targets
    for copy in copies[:8]:
        copy.wait()
    ints[...] = jnp.zeros((INTS, E), F32)
    ints[0:6, :] = neighbours[...].astype(F32)
    ints[8:14, :] = face_type[...].astype(F32)
    ints[14:15, :] = elem_type[...].astype(F32)
    ints[16:18, :NEAR] = near[...].astype(F32)
    ints[18:20, :FAR] = far[...].astype(F32)
    ints[20:21, :SUB] = sub[...].astype(F32)
    ints[21:22, :PAIRS] = pair[...].astype(F32)
    ints[22:23, :] = partner[...].astype(F32)
    message[2 * ROWS :, :] = ints[...].astype(BF)
    for i, field in enumerate((guess, rhs)):
        copies[8 + i].wait()
        blocks = [field[pl.ds(r, DOF, stride=RHS), :].astype(BF) for r in range(RHS)]
        message[i * ROWS : (i + 1) * ROWS, :] = jnp.concatenate(blocks, axis=0)
    for copy in copies[10:]:
        copy.wait()
    for d in range(FACES + 1):
        both = (diag[0], diag[1]) if d == 0 else (face[d - 1, 0], face[d - 1, 1])
        wide_ref[:, d * 2 * DOF : (d + 1) * 2 * DOF] = jnp.concatenate(both, axis=1)
    wide_ref[:, WIDE:] = jnp.concatenate([smooth[0], smooth[1]], axis=1)


def tables(lists, core, odd, local_ref, halo_ref, mask_ref):
    below = jnp.where(odd, 0, CROSS)
    above = jnp.where(odd, CROSS, 0)
    first = core == 0
    slots = []
    for d in range(FACES):
        k = lists[d : d + 1, :]
        m = k - 208
        place = 2 * CROSS + (m >> 3) * 2 * SUB + core * SUB + (m & 7)
        place = jnp.where(k < 208, above + NEAR + core * FAR + k - 200, place)
        place = jnp.where(k < 200, below + NEAR + core * FAR + k - 192, place)
        place = jnp.where(k < 192, jnp.where(first, -1, above + k - 160), place)
        place = jnp.where(k < 160, jnp.where(first, below + k - 128, -1), place)
        place = jnp.where(k < E, -1, place)
        lanes = slice(d * E, (d + 1) * E)
        local_ref[:, lanes] = jnp.where(iota((E, E), 0) == k, 1.0, 0.0).astype(BF)
        halo_ref[:, lanes] = jnp.where(iota((HALO, E), 0) == place, 1.0, 0.0).astype(BF)
        start = jnp.where(first, 160, 128)
        slots.append(jnp.where(iota((NEAR, E), 0) + start == k, 1.0, 0.0).astype(BF))
    for d in range(FACES + 1):
        kinds = lists[14:15, :] if d == 0 else lists[7 + d : 8 + d, :]
        for t in range(2):
            mask_ref[2 * d + t] = jnp.where(jnp.broadcast_to(kinds, (16, E)) == t, 1.0, 0.0).astype(BF)
    return jnp.concatenate(slots, axis=1)


def own_kernel(place_ref, mine, field_ref, ints_ref, slot_ref, local_ref, halo_ref, mask_ref):
    lists = mine[2 * ROWS :, :].astype(F32).astype(jnp.int32)
    ints_ref[...] = lists
    slot_ref[...] = tables(lists, place_ref[0], place_ref[1] == 1, local_ref, halo_ref, mask_ref)
    field_ref[...] = mine[:ROWS, :]


def pack_kernel(place_ref, own_field, own_lists, own_slots, other, field_ref, choice_ref, inner_ref, outer_ref, local_ref, halo_ref, mask_ref, *messages):
    core = place_ref[0]
    first = core == 0
    odd = place_ref[1] == 1
    mine = own_lists[...]
    theirs = other[2 * ROWS :, :].astype(F32).astype(jnp.int32)
    low = jnp.where(first, mine, theirs)
    high = jnp.where(first, theirs, mine)
    low_at, high_at = core * E, (1 - core) * E
    field = jnp.concatenate([own_field[...], other[:ROWS, :]], axis=1)

    def chosen(near, one, two):
        return picker(near, CHIP), jnp.concatenate([picker(one + low_at, CHIP), picker(two + high_at, CHIP)], axis=0)

    up = (high[17:18, :NEAR] + high_at, low[19:20, :FAR], high[19:20, :FAR])
    down = (low[16:17, :NEAR] + low_at, low[18:19, :FAR], high[18:19, :FAR])
    to_one = [jnp.where(odd, d, u) for u, d in zip(up, down)]
    to_two = [jnp.where(odd, u, d) for u, d in zip(up, down)]
    side = jnp.concatenate([picker(low[20:21, :SUB] + low_at, CHIP), picker(high[20:21, :SUB] + high_at, CHIP)], axis=0)
    choice = jnp.concatenate([*chosen(*to_one), *chosen(*to_two), side, side, side, side], axis=0)
    send(choice, field, zip(messages, (CROSS, CROSS, SIDE)))
    choice_ref[...] = choice
    field_ref[...] = field
    their_slots = tables(theirs, 1 - core, odd, local_ref, halo_ref, mask_ref)
    listed = jnp.where(first, theirs[16:17, :NEAR], theirs[17:18, :NEAR])
    inner = jnp.where(iota((E, NEAR), 0) == listed, 1.0, 0.0).astype(BF)
    inner_ref[...] = jnp.dot(inner, own_slots[...], preferred_element_type=F32).astype(BF)
    listed = jnp.where(first, mine[17:18, :NEAR], mine[16:17, :NEAR])
    outer = jnp.where(iota((E, NEAR), 0) == listed, 1.0, 0.0).astype(BF)
    outer_ref[...] = jnp.dot(outer, their_slots, preferred_element_type=F32).astype(BF)


def masked(block, mask):
    return block * jnp.concatenate([mask] * (DOF // 16), axis=0)


def extend(field_ref, halo):
    near = jnp.concatenate([ref[:used] for ref, used in zip(halo, (CROSS, CROSS, SIDE))], axis=0)
    return jnp.concatenate([field_ref[...], near.T], axis=1)


def select(extended, *blocks):
    columns = jnp.concatenate([block[...] for block in blocks], axis=0)
    return jnp.dot(extended, columns, preferred_element_type=F32).astype(BF)


def sweep_kernel(field_ref, two, one, side, *refs):
    own_local, own_halo, own_masks, inner, outer, local, halo, masks, wide, rhs, other, choice, *refs = refs
    before, (after, next_field, *messages) = refs[:-5], refs[-5:]
    extended = extend(field_ref, (one, two, side))
    mine = select(extended, own_local, inner, own_halo)
    theirs = select(extended, outer, local, halo)
    kinds = [jnp.concatenate([own_masks[i], masks[i]], axis=1) for i in range(2 * FACES + 2)]
    parts = []
    for r in range(RHS):
        rows = slice(r * DOF, (r + 1) * DOF)
        stack = []
        for d in range(FACES + 1):
            lanes = slice((d - 1) * E, d * E)
            block = field_ref[rows, :] if d == 0 else jnp.concatenate([mine[rows, lanes], theirs[rows, lanes]], axis=1)
            stack += [masked(block, kinds[2 * d]), masked(block, kinds[2 * d + 1])]
        product = jnp.dot(wide[:, :WIDE], jnp.concatenate(stack, axis=0), preferred_element_type=F32)
        given = other[ROWS + r * DOF : ROWS + (r + 1) * DOF, :].astype(F32)
        given = jnp.concatenate([rhs[pl.ds(r, DOF, stride=RHS), :], given], axis=1)
        rounded = (given - product).astype(BF)
        parts.append(jnp.concatenate([masked(rounded, kinds[0]), masked(rounded, kinds[1])], axis=0))
    changes = jnp.concatenate([jnp.dot(wide[:, WIDE:], part, preferred_element_type=F32) for part in parts], axis=0)
    if len(before) == 1 and before[0].shape[1] == CHIP:
        old = field_ref[...].astype(F32) + before[0][...].astype(F32)
    else:
        own = jnp.concatenate([before[0][pl.ds(r, DOF, stride=RHS), :] for r in range(RHS)], axis=0)
        old = jnp.concatenate([own, other[:ROWS, :].astype(F32)], axis=1)
    new = old + changes
    rounded = new.astype(BF)
    send(choice[...], rounded, zip(messages, (CROSS, CROSS, SIDE)))
    after[...] = (new - rounded.astype(F32)).astype(BF)
    next_field[...] = rounded


def residual_kernel(field_ref, two, one, side, own_local, inner, own_halo, masks, wide, rhs, lists, residual_ref, rounded_ref, message):
    beside = select(extend(field_ref, (one, two, side)), own_local, inner, own_halo)
    parts = []
    for r in range(0, RHS, 2):
        halves = []
        for s in (r, r + 1):
            rows = slice(s * DOF, (s + 1) * DOF)
            stack = []
            for d in range(FACES + 1):
                block = field_ref[rows, :E] if d == 0 else beside[rows, (d - 1) * E : d * E]
                stack += [masked(block, masks[2 * d]), masked(block, masks[2 * d + 1])]
            halves.append(jnp.concatenate(stack, axis=0))
        product = jnp.dot(wide[:, :WIDE], jnp.concatenate(halves, axis=1), preferred_element_type=F32)
        parts += [rhs[pl.ds(r + i, DOF, stride=RHS), :] - product[:, i * E : (i + 1) * E] for i in range(2)]
    residual = jnp.concatenate(parts, axis=0)
    rounded = residual.astype(BF)
    send(picker(lists[21:22, :PAIRS], E), rounded, [(message, PAIRS)])
    residual_ref[...] = residual
    rounded_ref[...] = rounded


def mate_picker(partner, first, count):
    return jnp.where(iota((count, E), 0) + first == partner, 1.0, 0.0).astype(BF)


def local_kernel(residual_ref, rounded_ref, lists, out_ref, half_ref):
    residual = residual_ref[...]
    rounded = rounded_ref[...]
    rest = (residual - rounded.astype(F32)).astype(BF)
    local = mate_picker(lists[22:23, :], 0, E)
    mates = jnp.dot(rounded, local, preferred_element_type=F32)
    mates = mates + jnp.dot(rest, local, preferred_element_type=F32)
    for r in range(RHS):
        out_ref[pl.ds(r, DOF, stride=RHS), :] = residual[r * DOF : (r + 1) * DOF, :]
    half_ref[...] = residual + mates


def coarse_kernel(half_ref, incoming, lists, inverse, field_ref, rest, solution_ref):
    mates = lax.dot_general(
        incoming[...], mate_picker(lists[22:23, :], E, PAIRS), (((0,), (0,)), ((), ())), preferred_element_type=F32
    )
    coarse = (half_ref[...] + mates).astype(BF)
    solved = []
    for r in range(0, RHS, 2):
        pair = jnp.concatenate([coarse[s * DOF : (s + 1) * DOF, :] for s in (r, r + 1)], axis=1)
        update = jnp.dot(inverse[...], pair, preferred_element_type=F32)
        for i in range(2):
            rows = slice((r + i) * DOF, (r + i + 1) * DOF)
            iterate = field_ref[rows, :E].astype(F32) + rest[rows, :E].astype(F32)
            solved.append(iterate + update[:, i * E : (i + 1) * E])
    for r in range(RHS):
        solution_ref[pl.ds(r, DOF, stride=RHS), :] = solved[r]


def body(
    rhs,
    guess,
    diag_blocks,
    face_blocks,
    smoother,
    coarse_inverse,
    elem_type,
    face_type,
    neighbours,
    send_near,
    send_far,
    sub_send,
    partner,
    pair_send,
):
    a = lax.axis_index("dom")
    place = jnp.stack([a % 2, (a // 2) % 2]).astype(jnp.int32)
    doms = lax.axis_size("dom")
    rhs = rhs.reshape(ROWS, E)
    guess = guess.reshape(ROWS, E)
    inside = [(i, i + 1) for i in range(0, doms, 2)]
    cross_one = [(i + j, i + j + 2) for i in range(0, doms, 4) for j in range(2)]
    cross_two = [(i + j + 2, i + j + 4) for i in range(0, doms, 4) for j in range(2)]

    def exchange(messages):
        one, two, side = messages
        two = swap(two, "dom", cross_two)
        one = swap(one, "dom", cross_one)
        side = lax.all_to_all(side, "sub", 0, 0, tiled=True)
        return two, one, side

    message_outs = [((n, ROWS), BF) for n in SENT]
    taken = (send_near, send_far, sub_send.reshape(1, -1), elem_type.reshape(1, -1), face_type, neighbours)
    taken += (pair_send.reshape(1, -1), partner.reshape(1, -1), guess, rhs)
    taken += (diag_blocks, face_blocks, smoother)
    mine, wide = call(
        first_kernel,
        [((2 * ROWS + INTS, E), BF), ((DOF, WIDE + 2 * DOF), BF)],
        *taken,
        remote=len(taken),
        scratch=[pltpu.VMEM(x.shape, x.dtype) for x in taken]
        + [pltpu.VMEM((INTS, E), F32), pltpu.SemaphoreType.DMA((len(taken),))],
        vmem=60,
    )
    other = swap(mine, "dom", inside)
    table_outs = [((E, FACES * E), BF), ((HALO, FACES * E), BF), ((2 * FACES + 2, 16, E), BF)]
    own_field, own_lists, own_slots, own_local, own_halo, own_masks = call(
        own_kernel,
        [((ROWS, E), BF), ((INTS, E), jnp.int32), ((NEAR, FACES * E), BF)] + table_outs,
        place,
        mine,
        flops=1000000,
        scalars=1,
    )
    field, choice, inner, outer, local, halo, masks, *messages = call(
        pack_kernel,
        [((ROWS, CHIP), BF), ((HALO, CHIP), BF), ((E, FACES * E), BF), ((E, FACES * E), BF)] + table_outs + message_outs,
        place,
        own_field,
        own_lists,
        own_slots,
        other,
        flops=2 * HALO * CHIP * ROWS,
        scalars=1,
    )
    brought = exchange(messages)
    work = 2 * ROWS * (CHIP + HALO) * FACES * CHIP + 2 * DOF * 14 * DOF * RHS * CHIP
    iterate = guess
    for _ in range(SWEEPS):
        iterate, field, *messages = call(
            sweep_kernel,
            [((ROWS, CHIP), BF), ((ROWS, CHIP), BF)] + message_outs,
            field,
            *brought,
            own_local,
            own_halo,
            own_masks,
            inner,
            outer,
            local,
            halo,
            masks,
            wide,
            rhs,
            other,
            choice,
            iterate,
            flops=work,
        )
        brought = exchange(messages)
    residual, rounded, message = call(
        residual_kernel,
        [((ROWS, E), F32), ((ROWS, E), BF), ((PAIRS, ROWS), BF)],
        field,
        *brought,
        own_local,
        inner,
        own_halo,
        own_masks,
        wide,
        rhs,
        own_lists,
        flops=work // 2,
    )
    subs = lax.axis_size("sub")
    incoming = swap(message, "sub", [(i, i + 1) for i in range(0, subs, 2)])
    residual, coarse = call(
        local_kernel,
        [((ROWS, E), F32), ((ROWS, E), F32)],
        residual,
        rounded,
        own_lists,
        flops=work // 8,
    )
    (solved,) = call(
        coarse_kernel,
        [((ROWS, E), F32)],
        coarse,
        incoming,
        own_lists,
        coarse_inverse,
        field,
        iterate,
        flops=work // 8,
    )
    shape = (DOF, RHS, E)
    return (solved.reshape(shape), residual.reshape(shape))


SENT = (CROSS, CROSS, SIDE)


def solution(mesh):
    block = P(None, None, ("dom", "sub"))
    flat = P(("dom", "sub"))
    listed = P(None, ("dom", "sub"))
    in_specs = (block, block, P(), P(), P(), P(), flat, listed, listed, listed, listed, flat, flat, flat)
    return jax.shard_map(body, mesh=mesh, in_specs=in_specs, out_specs=(block, block), check_vma=False)
```

```python
import jax
import jax.numpy as jnp
from jax import lax
from jax.experimental import pallas as pl
from jax.experimental.pallas import tpu as pltpu
from jax.sharding import PartitionSpec as P

SWEEPS = 2
DOF = 64
RHS = 8
E = 128
CHIP = 2 * E
FACES = 6
ROWS = DOF * RHS
NEAR = 32
FAR = 8
SUB = 8
PAIRS = 16
CROSS = NEAR + 2 * FAR
SIDE = 4 * 2 * SUB
HALO = 2 * CROSS + SIDE
WIDE = 2 * DOF * (FACES + 1)
INTS = 32
BF = jnp.bfloat16
F32 = jnp.float32


def swap(array, axis, pairs):
    count = lax.axis_size(axis)
    route = []
    for low, high in pairs:
        if high < count:
            route += [(low, high), (high, low)]
    return lax.ppermute(array, axis, route)


def spec():
    return pl.BlockSpec(memory_space=pltpu.VMEM)


def call(kernel, outs, *args, flops=0, scalars=0, remote=0, scratch=(), vmem=16):
    specs = [pl.BlockSpec(memory_space=pltpu.SMEM)] * scalars
    specs += [pl.BlockSpec(memory_space=pl.ANY)] * remote
    specs += [spec()] * (len(args) - scalars - remote)
    moved = sum(a.size * a.dtype.itemsize for a in args)
    return pl.pallas_call(
        kernel,
        out_shape=[jax.ShapeDtypeStruct(s, d) for s, d in outs],
        in_specs=specs,
        out_specs=[spec()] * len(outs),
        scratch_shapes=scratch,
        cost_estimate=pl.CostEstimate(flops=flops, bytes_accessed=moved, transcendentals=0),
        compiler_params=pltpu.CompilerParams(vmem_limit_bytes=vmem << 20),
    )(*args)


def iota(shape, dim):
    return lax.broadcasted_iota(jnp.int32, shape, dim)


def column(row):
    count = row.shape[1]
    wide = jnp.broadcast_to(row.astype(F32), (count, count))
    kept = jnp.where(iota((count, count), 0) == iota((count, count), 1), wide, 0.0)
    return jnp.sum(kept, axis=1, keepdims=True).astype(jnp.int32)


def picker(row, width):
    count = row.shape[1]
    return jnp.where(iota((count, width), 1) == column(row), 1.0, 0.0).astype(BF)


def send(choice, field, refs):
    rows = lax.dot_general(choice, field, (((1,), (1,)), ((), ())), preferred_element_type=F32).astype(BF)
    start = 0
    for ref, used in refs:
        ref[:used] = rows[start : start + used]
        if ref.shape[0] > used:
            ref[used:] = jnp.zeros((ref.shape[0] - used, ROWS), BF)
        start += used


def first_kernel(*refs):
    sources, (message, wide_ref), targets, (ints, arrived) = refs[:13], refs[13:15], refs[15:28], refs[28:]
    copies = [pltpu.make_async_copy(a, b, arrived.at[i]) for i, (a, b) in enumerate(zip(sources, targets))]
    for copy in copies[8:10] + copies[:8] + copies[10:]:
        copy.start()
    near, far, sub, elem_type, face_type, neighbours, pair, partner, guess, rhs, diag, face, smooth = targets
    for copy in copies[:8]:
        copy.wait()
    ints[...] = jnp.zeros((INTS, E), F32)
    ints[0:6, :] = neighbours[...].astype(F32)
    ints[8:14, :] = face_type[...].astype(F32)
    ints[14:15, :] = elem_type[...].astype(F32)
    ints[16:18, :NEAR] = near[...].astype(F32)
    ints[18:20, :FAR] = far[...].astype(F32)
    ints[20:21, :SUB] = sub[...].astype(F32)
    ints[21:22, :PAIRS] = pair[...].astype(F32)
    ints[22:23, :] = partner[...].astype(F32)
    message[2 * ROWS :, :] = ints[...].astype(BF)
    for copy in copies[10:]:
        copy.wait()
    for d in range(FACES + 1):
        both = (diag[0], diag[1]) if d == 0 else (face[d - 1, 0], face[d - 1, 1])
        wide_ref[:, d * 2 * DOF : (d + 1) * 2 * DOF] = jnp.concatenate(both, axis=1)
    wide_ref[:, WIDE:] = jnp.concatenate([smooth[0], smooth[1]], axis=1)
    for i, field in enumerate((guess, rhs)):
        copies[8 + i].wait()
        blocks = [field[pl.ds(r, DOF, stride=RHS), :].astype(BF) for r in range(RHS)]
        message[i * ROWS : (i + 1) * ROWS, :] = jnp.concatenate(blocks, axis=0)


def tables(lists, core, odd, local_ref, halo_ref, mask_ref):
    below = jnp.where(odd, 0, CROSS)
    above = jnp.where(odd, CROSS, 0)
    first = core == 0
    slots = []
    for d in range(FACES):
        k = lists[d : d + 1, :]
        m = k - 208
        place = 2 * CROSS + (m >> 3) * 2 * SUB + core * SUB + (m & 7)
        place = jnp.where(k < 208, above + NEAR + core * FAR + k - 200, place)
        place = jnp.where(k < 200, below + NEAR + core * FAR + k - 192, place)
        place = jnp.where(k < 192, jnp.where(first, -1, above + k - 160), place)
        place = jnp.where(k < 160, jnp.where(first, below + k - 128, -1), place)
        place = jnp.where(k < E, -1, place)
        lanes = slice(d * E, (d + 1) * E)
        local_ref[:, lanes] = jnp.where(iota((E, E), 0) == k, 1.0, 0.0).astype(BF)
        halo_ref[:, lanes] = jnp.where(iota((HALO, E), 0) == place, 1.0, 0.0).astype(BF)
        start = jnp.where(first, 160, 128)
        slots.append(jnp.where(iota((NEAR, E), 0) + start == k, 1.0, 0.0).astype(BF))
    for d in range(FACES + 1):
        kinds = lists[14:15, :] if d == 0 else lists[7 + d : 8 + d, :]
        for t in range(2):
            mask_ref[2 * d + t] = jnp.where(jnp.broadcast_to(kinds, (16, E)) == t, 1.0, 0.0).astype(BF)
    return jnp.concatenate(slots, axis=1)


def own_kernel(place_ref, mine, field_ref, ints_ref, slot_ref, local_ref, halo_ref, mask_ref):
    lists = mine[2 * ROWS :, :].astype(F32).astype(jnp.int32)
    ints_ref[...] = lists
    slot_ref[...] = tables(lists, place_ref[0], place_ref[1] == 1, local_ref, halo_ref, mask_ref)
    field_ref[...] = mine[:ROWS, :]


def pack_kernel(place_ref, own_field, own_lists, own_slots, other, field_ref, choice_ref, inner_ref, outer_ref, local_ref, halo_ref, mask_ref, *messages):
    core = place_ref[0]
    first = core == 0
    odd = place_ref[1] == 1
    mine = own_lists[...]
    theirs = other[2 * ROWS :, :].astype(F32).astype(jnp.int32)
    low = jnp.where(first, mine, theirs)
    high = jnp.where(first, theirs, mine)
    low_at, high_at = core * E, (1 - core) * E
    field = jnp.concatenate([own_field[...], other[:ROWS, :]], axis=1)

    def chosen(near, one, two):
        return picker(near, CHIP), jnp.concatenate([picker(one + low_at, CHIP), picker(two + high_at, CHIP)], axis=0)

    up = (high[17:18, :NEAR] + high_at, low[19:20, :FAR], high[19:20, :FAR])
    down = (low[16:17, :NEAR] + low_at, low[18:19, :FAR], high[18:19, :FAR])
    to_one = [jnp.where(odd, d, u) for u, d in zip(up, down)]
    to_two = [jnp.where(odd, u, d) for u, d in zip(up, down)]
    side = jnp.concatenate([picker(low[20:21, :SUB] + low_at, CHIP), picker(high[20:21, :SUB] + high_at, CHIP)], axis=0)
    choice = jnp.concatenate([*chosen(*to_one), *chosen(*to_two), side, side, side, side], axis=0)
    send(choice, field, zip(messages, (CROSS, CROSS, SIDE)))
    choice_ref[...] = choice
    field_ref[...] = field
    their_slots = tables(theirs, 1 - core, odd, local_ref, halo_ref, mask_ref)
    listed = jnp.where(first, theirs[16:17, :NEAR], theirs[17:18, :NEAR])
    inner = jnp.where(iota((E, NEAR), 0) == listed, 1.0, 0.0).astype(BF)
    inner_ref[...] = jnp.dot(inner, own_slots[...], preferred_element_type=F32).astype(BF)
    listed = jnp.where(first, mine[17:18, :NEAR], mine[16:17, :NEAR])
    outer = jnp.where(iota((E, NEAR), 0) == listed, 1.0, 0.0).astype(BF)
    outer_ref[...] = jnp.dot(outer, their_slots, preferred_element_type=F32).astype(BF)


def masked(block, mask):
    return block * jnp.concatenate([mask] * (DOF // 16), axis=0)


def extend(field_ref, halo):
    near = jnp.concatenate([ref[:used] for ref, used in zip(halo, (CROSS, CROSS, SIDE))], axis=0)
    return jnp.concatenate([field_ref[...], near.T], axis=1)


def select(extended, *blocks):
    columns = jnp.concatenate([block[...] for block in blocks], axis=0)
    return jnp.dot(extended, columns, preferred_element_type=F32).astype(BF)


def sweep_kernel(field_ref, two, one, side, *refs):
    own_local, own_halo, own_masks, inner, outer, local, halo, masks, wide, rhs, other, choice, *refs = refs
    before, (after, next_field, *messages) = refs[:-5], refs[-5:]
    extended = extend(field_ref, (one, two, side))
    mine = select(extended, own_local, inner, own_halo)
    theirs = select(extended, outer, local, halo)
    kinds = [jnp.concatenate([own_masks[i], masks[i]], axis=1) for i in range(2 * FACES + 2)]
    parts = []
    for r in range(RHS):
        rows = slice(r * DOF, (r + 1) * DOF)
        stack = []
        for d in range(FACES + 1):
            lanes = slice((d - 1) * E, d * E)
            block = field_ref[rows, :] if d == 0 else jnp.concatenate([mine[rows, lanes], theirs[rows, lanes]], axis=1)
            stack += [masked(block, kinds[2 * d]), masked(block, kinds[2 * d + 1])]
        product = jnp.dot(wide[:, :WIDE], jnp.concatenate(stack, axis=0), preferred_element_type=F32)
        given = other[ROWS + r * DOF : ROWS + (r + 1) * DOF, :].astype(F32)
        given = jnp.concatenate([rhs[pl.ds(r, DOF, stride=RHS), :], given], axis=1)
        rounded = (given - product).astype(BF)
        parts.append(jnp.concatenate([masked(rounded, kinds[0]), masked(rounded, kinds[1])], axis=0))
    changes = jnp.concatenate([jnp.dot(wide[:, WIDE:], part, preferred_element_type=F32) for part in parts], axis=0)
    if len(before) == 1 and before[0].shape[1] == CHIP:
        old = before[0][...]
    else:
        own = jnp.concatenate([before[0][pl.ds(r, DOF, stride=RHS), :] for r in range(RHS)], axis=0)
        old = jnp.concatenate([own, other[:ROWS, :].astype(F32)], axis=1)
    new = old + changes
    rounded = new.astype(BF)
    send(choice[...], rounded, zip(messages, (CROSS, CROSS, SIDE)))
    after[...] = new
    next_field[...] = rounded


def residual_kernel(field_ref, two, one, side, own_local, inner, own_halo, masks, wide, rhs, lists, residual_ref, rounded_ref, message):
    beside = select(extend(field_ref, (one, two, side)), own_local, inner, own_halo)
    parts = []
    for r in range(0, RHS, 2):
        halves = []
        for s in (r, r + 1):
            rows = slice(s * DOF, (s + 1) * DOF)
            stack = []
            for d in range(FACES + 1):
                block = field_ref[rows, :E] if d == 0 else beside[rows, (d - 1) * E : d * E]
                stack += [masked(block, masks[2 * d]), masked(block, masks[2 * d + 1])]
            halves.append(jnp.concatenate(stack, axis=0))
        product = jnp.dot(wide[:, :WIDE], jnp.concatenate(halves, axis=1), preferred_element_type=F32)
        parts += [rhs[pl.ds(r + i, DOF, stride=RHS), :] - product[:, i * E : (i + 1) * E] for i in range(2)]
    residual = jnp.concatenate(parts, axis=0)
    rounded = residual.astype(BF)
    send(picker(lists[21:22, :PAIRS], E), rounded, [(message, PAIRS)])
    residual_ref[...] = residual
    rounded_ref[...] = rounded


def mate_picker(partner, first, count):
    return jnp.where(iota((count, E), 0) + first == partner, 1.0, 0.0).astype(BF)


def local_kernel(residual_ref, rounded_ref, lists, out_ref, half_ref):
    residual = residual_ref[...]
    rounded = rounded_ref[...]
    rest = (residual - rounded.astype(F32)).astype(BF)
    local = mate_picker(lists[22:23, :], 0, E)
    mates = jnp.dot(rounded, local, preferred_element_type=F32)
    mates = mates + jnp.dot(rest, local, preferred_element_type=F32)
    for r in range(RHS):
        out_ref[pl.ds(r, DOF, stride=RHS), :] = residual[r * DOF : (r + 1) * DOF, :]
    half_ref[...] = residual + mates


def coarse_kernel(half_ref, incoming, lists, inverse, iterate, solution_ref):
    mates = lax.dot_general(
        incoming[...], mate_picker(lists[22:23, :], E, PAIRS), (((0,), (0,)), ((), ())), preferred_element_type=F32
    )
    coarse = (half_ref[...] + mates).astype(BF)
    solved = []
    for r in range(0, RHS, 2):
        pair = jnp.concatenate([coarse[s * DOF : (s + 1) * DOF, :] for s in (r, r + 1)], axis=1)
        update = jnp.dot(inverse[...], pair, preferred_element_type=F32)
        solved += [iterate[(r + i) * DOF : (r + i + 1) * DOF, :E] + update[:, i * E : (i + 1) * E] for i in range(2)]
    for r in range(RHS):
        solution_ref[pl.ds(r, DOF, stride=RHS), :] = solved[r]


def body(
    rhs,
    guess,
    diag_blocks,
    face_blocks,
    smoother,
    coarse_inverse,
    elem_type,
    face_type,
    neighbours,
    send_near,
    send_far,
    sub_send,
    partner,
    pair_send,
):
    a = lax.axis_index("dom")
    place = jnp.stack([a % 2, (a // 2) % 2]).astype(jnp.int32)
    doms = lax.axis_size("dom")
    rhs = rhs.reshape(ROWS, E)
    guess = guess.reshape(ROWS, E)
    inside = [(i, i + 1) for i in range(0, doms, 2)]
    cross_one = [(i + j, i + j + 2) for i in range(0, doms, 4) for j in range(2)]
    cross_two = [(i + j + 2, i + j + 4) for i in range(0, doms, 4) for j in range(2)]

    def exchange(messages):
        one, two, side = messages
        two = swap(two, "dom", cross_two)
        one = swap(one, "dom", cross_one)
        side = lax.all_to_all(side, "sub", 0, 0, tiled=True)
        return two, one, side

    message_outs = [((n, ROWS), BF) for n in SENT]
    taken = (send_near, send_far, sub_send.reshape(1, -1), elem_type.reshape(1, -1), face_type, neighbours)
    taken += (pair_send.reshape(1, -1), partner.reshape(1, -1), guess, rhs)
    taken += (diag_blocks, face_blocks, smoother)
    mine, wide = call(
        first_kernel,
        [((2 * ROWS + INTS, E), BF), ((DOF, WIDE + 2 * DOF), BF)],
        *taken,
        remote=len(taken),
        scratch=[pltpu.VMEM(x.shape, x.dtype) for x in taken]
        + [pltpu.VMEM((INTS, E), F32), pltpu.SemaphoreType.DMA((len(taken),))],
        vmem=60,
    )
    other = swap(mine, "dom", inside)
    table_outs = [((E, FACES * E), BF), ((HALO, FACES * E), BF), ((2 * FACES + 2, 16, E), BF)]
    own_field, own_lists, own_slots, own_local, own_halo, own_masks = call(
        own_kernel,
        [((ROWS, E), BF), ((INTS, E), jnp.int32), ((NEAR, FACES * E), BF)] + table_outs,
        place,
        mine,
        flops=1000000,
        scalars=1,
    )
    field, choice, inner, outer, local, halo, masks, *messages = call(
        pack_kernel,
        [((ROWS, CHIP), BF), ((HALO, CHIP), BF), ((E, FACES * E), BF), ((E, FACES * E), BF)] + table_outs + message_outs,
        place,
        own_field,
        own_lists,
        own_slots,
        other,
        flops=2 * HALO * CHIP * ROWS,
        scalars=1,
    )
    brought = exchange(messages)
    work = 2 * ROWS * (CHIP + HALO) * FACES * CHIP + 2 * DOF * 14 * DOF * RHS * CHIP
    iterate = guess
    for _ in range(SWEEPS):
        iterate, field, *messages = call(
            sweep_kernel,
            [((ROWS, CHIP), F32), ((ROWS, CHIP), BF)] + message_outs,
            field,
            *brought,
            own_local,
            own_halo,
            own_masks,
            inner,
            outer,
            local,
            halo,
            masks,
            wide,
            rhs,
            other,
            choice,
            iterate,
            flops=work,
        )
        brought = exchange(messages)
    residual, rounded, message = call(
        residual_kernel,
        [((ROWS, E), F32), ((ROWS, E), BF), ((PAIRS, ROWS), BF)],
        field,
        *brought,
        own_local,
        inner,
        own_halo,
        own_masks,
        wide,
        rhs,
        own_lists,
        flops=work // 2,
    )
    subs = lax.axis_size("sub")
    incoming = swap(message, "sub", [(i, i + 1) for i in range(0, subs, 2)])
    residual, coarse = call(
        local_kernel,
        [((ROWS, E), F32), ((ROWS, E), F32)],
        residual,
        rounded,
        own_lists,
        flops=work // 8,
    )
    (solved,) = call(
        coarse_kernel,
        [((ROWS, E), F32)],
        coarse,
        incoming,
        own_lists,
        coarse_inverse,
        iterate,
        flops=work // 8,
    )
    shape = (DOF, RHS, E)
    return (solved.reshape(shape), residual.reshape(shape))


SENT = (SIDE, SIDE, SIDE)


def solution(mesh):
    block = P(None, None, ("dom", "sub"))
    flat = P(("dom", "sub"))
    listed = P(None, ("dom", "sub"))
    in_specs = (block, block, P(), P(), P(), P(), flat, listed, listed, listed, listed, flat, flat, flat)
    return jax.shard_map(body, mesh=mesh, in_specs=in_specs, out_specs=(block, block), check_vma=False)
```

```python
import jax
import jax.numpy as jnp
from jax import lax
from jax.experimental import pallas as pl
from jax.experimental.pallas import tpu as pltpu
from jax.sharding import PartitionSpec as P

SWEEPS = 2
DOF = 64
RHS = 8
E = 128
CHIP = 2 * E
FACES = 6
ROWS = DOF * RHS
NEAR = 32
FAR = 8
SUB = 8
PAIRS = 16
CROSS = NEAR + 2 * FAR
SIDE = 4 * 2 * SUB
HALO = 2 * CROSS + SIDE
WIDE = 2 * DOF * (FACES + 1)
INTS = 32
BF = jnp.bfloat16
F32 = jnp.float32


def swap(array, axis, pairs):
    count = lax.axis_size(axis)
    route = []
    for low, high in pairs:
        if high < count:
            route += [(low, high), (high, low)]
    return lax.ppermute(array, axis, route)


def spec():
    return pl.BlockSpec(memory_space=pltpu.VMEM)


def call(kernel, outs, *args, flops=0, scalars=0, remote=0, scratch=(), vmem=16):
    specs = [pl.BlockSpec(memory_space=pltpu.SMEM)] * scalars
    specs += [pl.BlockSpec(memory_space=pl.ANY)] * remote
    specs += [spec()] * (len(args) - scalars - remote)
    moved = sum(a.size * a.dtype.itemsize for a in args)
    return pl.pallas_call(
        kernel,
        out_shape=[jax.ShapeDtypeStruct(s, d) for s, d in outs],
        in_specs=specs,
        out_specs=[spec()] * len(outs),
        scratch_shapes=scratch,
        cost_estimate=pl.CostEstimate(flops=flops, bytes_accessed=moved, transcendentals=0),
        compiler_params=pltpu.CompilerParams(vmem_limit_bytes=vmem << 20),
    )(*args)


def iota(shape, dim):
    return lax.broadcasted_iota(jnp.int32, shape, dim)


def column(row):
    count = row.shape[1]
    wide = jnp.broadcast_to(row.astype(F32), (count, count))
    kept = jnp.where(iota((count, count), 0) == iota((count, count), 1), wide, 0.0)
    return jnp.sum(kept, axis=1, keepdims=True).astype(jnp.int32)


def picker(row, width):
    count = row.shape[1]
    return jnp.where(iota((count, width), 1) == column(row), 1.0, 0.0).astype(BF)


def send(choice, field, refs):
    rows = lax.dot_general(choice, field, (((1,), (1,)), ((), ())), preferred_element_type=F32).astype(BF)
    start = 0
    for ref, used in refs:
        ref[:used] = rows[start : start + used]
        if ref.shape[0] > used:
            ref[used:] = jnp.zeros((ref.shape[0] - used, ROWS), BF)
        start += used


def first_kernel(*refs):
    sources, (message, wide_ref), targets, (ints, arrived) = refs[:13], refs[13:15], refs[15:28], refs[28:]
    copies = [pltpu.make_async_copy(a, b, arrived.at[i]) for i, (a, b) in enumerate(zip(sources, targets))]
    for copy in copies[8:10] + copies[:8] + copies[10:]:
        copy.start()
    near, far, sub, elem_type, face_type, neighbours, pair, partner, guess, rhs, diag, face, smooth = targets
    for copy in copies[:8]:
        copy.wait()
    ints[...] = jnp.zeros((INTS, E), F32)
    ints[0:6, :] = neighbours[...].astype(F32)
    ints[8:14, :] = face_type[...].astype(F32)
    ints[14:15, :] = elem_type[...].astype(F32)
    ints[16:18, :NEAR] = near[...].astype(F32)
    ints[18:20, :FAR] = far[...].astype(F32)
    ints[20:21, :SUB] = sub[...].astype(F32)
    ints[21:22, :PAIRS] = pair[...].astype(F32)
    ints[22:23, :] = partner[...].astype(F32)
    message[2 * ROWS :, :] = ints[...].astype(BF)
    for i, field in enumerate((guess, rhs)):
        copies[8 + i].wait()
        blocks = [field[pl.ds(r, DOF, stride=RHS), :].astype(BF) for r in range(RHS)]
        message[i * ROWS : (i + 1) * ROWS, :] = jnp.concatenate(blocks, axis=0)
    for copy in copies[10:]:
        copy.wait()
    for d in range(FACES + 1):
        both = (diag[0], diag[1]) if d == 0 else (face[d - 1, 0], face[d - 1, 1])
        wide_ref[:, d * 2 * DOF : (d + 1) * 2 * DOF] = jnp.concatenate(both, axis=1)
    wide_ref[:, WIDE:] = jnp.concatenate([smooth[0], smooth[1]], axis=1)


def tables(lists, core, odd, local_ref, halo_ref, mask_ref):
    below = jnp.where(odd, 0, CROSS)
    above = jnp.where(odd, CROSS, 0)
    first = core == 0
    slots = []
    for d in range(FACES):
        k = lists[d : d + 1, :]
        m = k - 208
        place = 2 * CROSS + (m >> 3) * 2 * SUB + core * SUB + (m & 7)
        place = jnp.where(k < 208, above + NEAR + core * FAR + k - 200, place)
        place = jnp.where(k < 200, below + NEAR + core * FAR + k - 192, place)
        place = jnp.where(k < 192, jnp.where(first, -1, above + k - 160), place)
        place = jnp.where(k < 160, jnp.where(first, below + k - 128, -1), place)
        place = jnp.where(k < E, -1, place)
        lanes = slice(d * E, (d + 1) * E)
        local_ref[:, lanes] = jnp.where(iota((E, E), 0) == k, 1.0, 0.0).astype(BF)
        halo_ref[:, lanes] = jnp.where(iota((HALO, E), 0) == place, 1.0, 0.0).astype(BF)
        start = jnp.where(first, 160, 128)
        slots.append(jnp.where(iota((NEAR, E), 0) + start == k, 1.0, 0.0).astype(BF))
    for d in range(FACES + 1):
        kinds = lists[14:15, :] if d == 0 else lists[7 + d : 8 + d, :]
        for t in range(2):
            mask_ref[2 * d + t] = jnp.where(jnp.broadcast_to(kinds, (16, E)) == t, 1.0, 0.0).astype(BF)
    return jnp.concatenate(slots, axis=1)


def own_kernel(place_ref, mine, field_ref, ints_ref, slot_ref, local_ref, halo_ref, mask_ref):
    lists = mine[2 * ROWS :, :].astype(F32).astype(jnp.int32)
    ints_ref[...] = lists
    slot_ref[...] = tables(lists, place_ref[0], place_ref[1] == 1, local_ref, halo_ref, mask_ref)
    field_ref[...] = mine[:ROWS, :]


def pack_kernel(place_ref, own_field, own_lists, own_slots, other, field_ref, choice_ref, inner_ref, outer_ref, local_ref, halo_ref, mask_ref, *messages):
    core = place_ref[0]
    first = core == 0
    odd = place_ref[1] == 1
    mine = own_lists[...]
    theirs = other[2 * ROWS :, :].astype(F32).astype(jnp.int32)
    low = jnp.where(first, mine, theirs)
    high = jnp.where(first, theirs, mine)
    low_at, high_at = core * E, (1 - core) * E
    field = jnp.concatenate([own_field[...], other[:ROWS, :]], axis=1)

    def chosen(near, one, two):
        return picker(near, CHIP), jnp.concatenate([picker(one + low_at, CHIP), picker(two + high_at, CHIP)], axis=0)

    up = (high[17:18, :NEAR] + high_at, low[19:20, :FAR], high[19:20, :FAR])
    down = (low[16:17, :NEAR] + low_at, low[18:19, :FAR], high[18:19, :FAR])
    to_one = [jnp.where(odd, d, u) for u, d in zip(up, down)]
    to_two = [jnp.where(odd, u, d) for u, d in zip(up, down)]
    side = jnp.concatenate([picker(low[20:21, :SUB] + low_at, CHIP), picker(high[20:21, :SUB] + high_at, CHIP)], axis=0)
    choice = jnp.concatenate([*chosen(*to_one), *chosen(*to_two), side, side, side, side], axis=0)
    send(choice, field, zip(messages, (CROSS, CROSS, SIDE)))
    choice_ref[...] = choice
    field_ref[...] = field
    their_slots = tables(theirs, 1 - core, odd, local_ref, halo_ref, mask_ref)
    listed = jnp.where(first, theirs[16:17, :NEAR], theirs[17:18, :NEAR])
    inner = jnp.where(iota((E, NEAR), 0) == listed, 1.0, 0.0).astype(BF)
    inner_ref[...] = jnp.dot(inner, own_slots[...], preferred_element_type=F32).astype(BF)
    listed = jnp.where(first, mine[17:18, :NEAR], mine[16:17, :NEAR])
    outer = jnp.where(iota((E, NEAR), 0) == listed, 1.0, 0.0).astype(BF)
    outer_ref[...] = jnp.dot(outer, their_slots, preferred_element_type=F32).astype(BF)


def masked(block, mask):
    return block * jnp.concatenate([mask] * (DOF // 16), axis=0)


def extend(field_ref, halo):
    near = jnp.concatenate([ref[:used] for ref, used in zip(halo, (CROSS, CROSS, SIDE))], axis=0)
    return jnp.concatenate([field_ref[...], near.T], axis=1)


def select(extended, *blocks):
    columns = jnp.concatenate([block[...] for block in blocks], axis=0)
    return jnp.dot(extended, columns, preferred_element_type=F32).astype(BF)


def sweep_kernel(field_ref, two, one, side, *refs):
    own_local, own_halo, own_masks, inner, outer, local, halo, masks, wide, rhs, other, choice, *refs = refs
    before, (after, next_field, *messages) = refs[:-5], refs[-5:]
    extended = extend(field_ref, (one, two, side))
    mine = select(extended, own_local, inner, own_halo)
    theirs = select(extended, outer, local, halo)
    kinds = [jnp.concatenate([own_masks[i], masks[i]], axis=1) for i in range(2 * FACES + 2)]
    parts = []
    for r in range(RHS):
        rows = slice(r * DOF, (r + 1) * DOF)
        stack = []
        for d in range(FACES + 1):
            lanes = slice((d - 1) * E, d * E)
            block = field_ref[rows, :] if d == 0 else jnp.concatenate([mine[rows, lanes], theirs[rows, lanes]], axis=1)
            stack += [masked(block, kinds[2 * d]), masked(block, kinds[2 * d + 1])]
        product = jnp.dot(wide[:, :WIDE], jnp.concatenate(stack, axis=0), preferred_element_type=F32)
        given = other[ROWS + r * DOF : ROWS + (r + 1) * DOF, :].astype(F32)
        given = jnp.concatenate([rhs[pl.ds(r, DOF, stride=RHS), :], given], axis=1)
        rounded = (given - product).astype(BF)
        parts.append(jnp.concatenate([masked(rounded, kinds[0]), masked(rounded, kinds[1])], axis=0))
    changes = jnp.concatenate([jnp.dot(wide[:, WIDE:], part, preferred_element_type=F32) for part in parts], axis=0)
    if len(before) == 1 and before[0].shape[1] == CHIP:
        old = before[0][...]
    else:
        own = jnp.concatenate([before[0][pl.ds(r, DOF, stride=RHS), :] for r in range(RHS)], axis=0)
        old = jnp.concatenate([own, other[:ROWS, :].astype(F32)], axis=1)
    new = old + changes
    rounded = new.astype(BF)
    send(choice[...], rounded, zip(messages, (CROSS, CROSS, SIDE)))
    after[...] = new
    next_field[...] = rounded


def residual_kernel(field_ref, two, one, side, own_local, inner, own_halo, masks, wide, rhs, lists, residual_ref, rounded_ref, message):
    beside = select(extend(field_ref, (one, two, side)), own_local, inner, own_halo)
    parts = []
    for r in range(0, RHS, 2):
        halves = []
        for s in (r, r + 1):
            rows = slice(s * DOF, (s + 1) * DOF)
            stack = []
            for d in range(FACES + 1):
                block = field_ref[rows, :E] if d == 0 else beside[rows, (d - 1) * E : d * E]
                stack += [masked(block, masks[2 * d]), masked(block, masks[2 * d + 1])]
            halves.append(jnp.concatenate(stack, axis=0))
        product = jnp.dot(wide[:, :WIDE], jnp.concatenate(halves, axis=1), preferred_element_type=F32)
        parts += [rhs[pl.ds(r + i, DOF, stride=RHS), :] - product[:, i * E : (i + 1) * E] for i in range(2)]
    residual = jnp.concatenate(parts, axis=0)
    rounded = residual.astype(BF)
    send(picker(lists[21:22, :PAIRS], E), rounded, [(message, PAIRS)])
    residual_ref[...] = residual
    rounded_ref[...] = rounded


def mate_picker(partner, first, count):
    return jnp.where(iota((count, E), 0) + first == partner, 1.0, 0.0).astype(BF)


def local_kernel(residual_ref, rounded_ref, lists, out_ref, half_ref):
    residual = residual_ref[...]
    rounded = rounded_ref[...]
    rest = (residual - rounded.astype(F32)).astype(BF)
    local = mate_picker(lists[22:23, :], 0, E)
    mates = jnp.dot(rounded, local, preferred_element_type=F32)
    mates = mates + jnp.dot(rest, local, preferred_element_type=F32)
    for r in range(RHS):
        out_ref[pl.ds(r, DOF, stride=RHS), :] = residual[r * DOF : (r + 1) * DOF, :]
    half_ref[...] = residual + mates


def coarse_kernel(half_ref, incoming, lists, inverse, iterate, solution_ref):
    mates = lax.dot_general(
        incoming[...], mate_picker(lists[22:23, :], E, PAIRS), (((0,), (0,)), ((), ())), preferred_element_type=F32
    )
    coarse = (half_ref[...] + mates).astype(BF)
    solved = []
    for r in range(0, RHS, 2):
        pair = jnp.concatenate([coarse[s * DOF : (s + 1) * DOF, :] for s in (r, r + 1)], axis=1)
        update = jnp.dot(inverse[...], pair, preferred_element_type=F32)
        solved += [iterate[(r + i) * DOF : (r + i + 1) * DOF, :E] + update[:, i * E : (i + 1) * E] for i in range(2)]
    for r in range(RHS):
        solution_ref[pl.ds(r, DOF, stride=RHS), :] = solved[r]


def body(
    rhs,
    guess,
    diag_blocks,
    face_blocks,
    smoother,
    coarse_inverse,
    elem_type,
    face_type,
    neighbours,
    send_near,
    send_far,
    sub_send,
    partner,
    pair_send,
):
    a = lax.axis_index("dom")
    place = jnp.stack([a % 2, (a // 2) % 2]).astype(jnp.int32)
    doms = lax.axis_size("dom")
    rhs = rhs.reshape(ROWS, E)
    guess = guess.reshape(ROWS, E)
    inside = [(i, i + 1) for i in range(0, doms, 2)]
    cross_one = [(i + j, i + j + 2) for i in range(0, doms, 4) for j in range(2)]
    cross_two = [(i + j + 2, i + j + 4) for i in range(0, doms, 4) for j in range(2)]

    def exchange(messages):
        one, two, side = messages
        two = swap(two, "dom", cross_two)
        one = swap(one, "dom", cross_one)
        side = lax.all_to_all(side, "sub", 0, 0, tiled=True)
        return two, one, side

    message_outs = [((n, ROWS), BF) for n in SENT]
    taken = (send_near, send_far, sub_send.reshape(1, -1), elem_type.reshape(1, -1), face_type, neighbours)
    taken += (pair_send.reshape(1, -1), partner.reshape(1, -1), guess, rhs)
    taken += (diag_blocks, face_blocks, smoother)
    mine, wide = call(
        first_kernel,
        [((2 * ROWS + INTS, E), BF), ((DOF, WIDE + 2 * DOF), BF)],
        *taken,
        remote=len(taken),
        scratch=[pltpu.VMEM(x.shape, x.dtype) for x in taken]
        + [pltpu.VMEM((INTS, E), F32), pltpu.SemaphoreType.DMA((len(taken),))],
        vmem=60,
    )
    other = swap(mine, "dom", inside)
    table_outs = [((E, FACES * E), BF), ((HALO, FACES * E), BF), ((2 * FACES + 2, 16, E), BF)]
    own_field, own_lists, own_slots, own_local, own_halo, own_masks = call(
        own_kernel,
        [((ROWS, E), BF), ((INTS, E), jnp.int32), ((NEAR, FACES * E), BF)] + table_outs,
        place,
        mine,
        flops=1000000,
        scalars=1,
    )
    field, choice, inner, outer, local, halo, masks, *messages = call(
        pack_kernel,
        [((ROWS, CHIP), BF), ((HALO, CHIP), BF), ((E, FACES * E), BF), ((E, FACES * E), BF)] + table_outs + message_outs,
        place,
        own_field,
        own_lists,
        own_slots,
        other,
        flops=2 * HALO * CHIP * ROWS,
        scalars=1,
    )
    brought = exchange(messages)
    work = 2 * ROWS * (CHIP + HALO) * FACES * CHIP + 2 * DOF * 14 * DOF * RHS * CHIP
    iterate = guess
    for _ in range(SWEEPS):
        iterate, field, *messages = call(
            sweep_kernel,
            [((ROWS, CHIP), F32), ((ROWS, CHIP), BF)] + message_outs,
            field,
            *brought,
            own_local,
            own_halo,
            own_masks,
            inner,
            outer,
            local,
            halo,
            masks,
            wide,
            rhs,
            other,
            choice,
            iterate,
            flops=work,
        )
        brought = exchange(messages)
    residual, rounded, message = call(
        residual_kernel,
        [((ROWS, E), F32), ((ROWS, E), BF), ((PAIRS, ROWS), BF)],
        field,
        *brought,
        own_local,
        inner,
        own_halo,
        own_masks,
        wide,
        rhs,
        own_lists,
        flops=work // 2,
    )
    subs = lax.axis_size("sub")
    incoming = swap(message, "sub", [(i, i + 1) for i in range(0, subs, 2)])
    residual, coarse = call(
        local_kernel,
        [((ROWS, E), F32), ((ROWS, E), F32)],
        residual,
        rounded,
        own_lists,
        flops=work // 8,
    )
    (solved,) = call(
        coarse_kernel,
        [((ROWS, E), F32)],
        coarse,
        incoming,
        own_lists,
        coarse_inverse,
        iterate,
        flops=work // 8,
    )
    shape = (DOF, RHS, E)
    return (solved.reshape(shape), residual.reshape(shape))


SENT = (SIDE + 16, SIDE + 16, SIDE)


def solution(mesh):
    block = P(None, None, ("dom", "sub"))
    flat = P(("dom", "sub"))
    listed = P(None, ("dom", "sub"))
    in_specs = (block, block, P(), P(), P(), P(), flat, listed, listed, listed, listed, flat, flat, flat)
    return jax.shard_map(body, mesh=mesh, in_specs=in_specs, out_specs=(block, block), check_vma=False)
```
